32 devices in a mesh: lat: 4 (over y, core), lon: 8 (over z, x).
Axes of the slice: x: 2, y: 2, z: 4, core: 2. Of those that a mesh axis runs over, the one named last changes fastest.
Arguments:
- state: float32 [4, 80, 32, 1024], P(None, None, 'lat', 'lon'), may hold values from -4 to 4
- mixing: float32 [32, 1024], P('lat', 'lon'), may hold values from 0.2 to 5
- insolation: float32 [32, 1024], P('lat', 'lon'), may hold values from 0 to 1
- filter_rows: int32 [32], replicated, may hold values 0 or 1
- block_map: int32 [32, 1024], P('lat', 'lon'), may hold values from 0 to 32767, as said below
Outputs:
- state_out: float32 [4, 80, 32, 1024], P(None, None, 'lat', 'lon')
- block_heating: float32 [32, 80, 1024], P(('lat', 'lon'))
The draws below stay inside these ranges and needn't reach their ends.
Inputs may be any that keep to these rules, and one draw needn't show every extreme that they name: `block_map`: blocks are numbered like the devices of the lat+lon axes. The 1024 columns of every device's tile give exactly 32 columns to each block, and each block's 1024 slots are each named by exactly one column.
All inputs are finite; a program needn't handle non-finite values.
Results may differ from the reference program's by a relative error of at most 0.0001.
Values sent between devices are 32-bit elements; how exact they have to be, the bound alone decides.
A program may use at most 64 MiB of HBM per device.

```python
import math
import jax
import jax.numpy as jnp
from jax import lax

FIELDS = 4
LEV = 80
CLAT = 8
CLON = 128
STEPS = 2
KEEP = 64
NLAT = 32
NLON = 1024
N_LAT = 4
N_LON = 8


def draw_block_map(key, part):
    devices = N_LAT * N_LON
    columns = CLAT * CLON
    per_peer = columns // devices
    source_keys = jax.random.split(jax.random.fold_in(key, 11), devices)
    source_perms = jax.vmap(lambda single: jax.random.permutation(single, columns))(source_keys).astype(jnp.int32)
    target = source_perms // per_peer
    position = source_perms % per_peer
    source_ids = jnp.arange(devices, dtype=jnp.int32)[:, None]
    pair_index = source_ids * per_peer + position
    target_keys = jax.random.split(jax.random.fold_in(key, 12), devices)
    target_perms = jax.vmap(lambda single: jax.random.permutation(single, columns))(target_keys).astype(jnp.int32)
    slots = target_perms[target, pair_index]
    values = target * columns + slots
    shaped = values.reshape(N_LAT, N_LON, CLAT, CLON)
    return jnp.transpose(shaped, (0, 2, 1, 3)).reshape(N_LAT * CLAT, N_LON * CLON).astype(jnp.int32)


def plant(entries, rng, least, largest):
    shape = entries.shape
    spot = [jax.random.randint(jax.random.fold_in(rng, axis), (), 0, shape[axis]) for axis in range(len(shape))]
    entries = entries.at[tuple(spot)].set(least)
    longest = shape.index(max(shape))
    spot[longest] = (spot[longest] + 1) % shape[longest]
    return entries.at[tuple(spot)].set(largest)


def steps_of(rng, extent, cuts, low, largest):
    def one(axis_at, shards_of):
        steps = jax.random.uniform(jax.random.fold_in(jax.random.fold_in(rng, 6), axis_at), (shards_of,), jnp.float32, low / len(cuts), largest / len(cuts))
        return jnp.repeat(jnp.exp(steps), extent[axis_at] // shards_of).reshape((-1,) + (1,) * (len(extent) - axis_at - 1))

    loudness = one(*cuts[0])
    for cut in cuts[1:]:
        loudness = loudness * one(*cut)
    return loudness


def noise(stream_key, extent, spread, limit, shards=(), kind=jnp.bfloat16):
    values = spread * jax.random.normal(stream_key, extent, jnp.float32)
    if shards:
        values = values * steps_of(stream_key, extent, shards, -0.22, 0.18)
    return jnp.clip(values, -limit, limit).astype(kind)


def setup_inputs(seed: int = 0) -> dict:
    keys = jax.random.split(jax.random.key(seed), 6)
    return {
        "state": noise(keys[0], (FIELDS, LEV, NLAT, NLON), 1.0, 4.0, ((2, 4), (3, 8)), jnp.float32),
        "mixing": jnp.clip(jnp.exp(math.log(5.0) - 3.218876 * jax.random.uniform(keys[1], (NLAT, NLON), jnp.float32) ** steps_of(keys[1], (NLAT, NLON), ((0, 4), (1, 8)), -0.2, 0.2)), 0.2, 5.0),
        "insolation": jnp.clip(1.0 * jax.random.uniform(keys[2], (NLAT, NLON), jnp.float32) ** steps_of(keys[2], (NLAT, NLON), ((0, 4), (1, 8)), -0.2, 0.2), 0.0, 1.0),
        "filter_rows": plant((jax.random.randint(keys[3], (NLAT,), 0, 3) < 1).astype(jnp.int32), jax.random.fold_in(keys[3], 1), 0, 1),
        "block_map": draw_block_map(jax.random.fold_in(keys[5], 71), 0),
    }


ADVECT = 0.1
DIFFUSE = 0.1
ROTATE = 0.2
RADIATE = 0.5
FLOOR = 0.25


def advance(extended, row_index, total_rows):
    center = extended[:, :, 1:-1, 1:-1]
    eastern = extended[:, :, 1:-1, 2:]
    western = extended[:, :, 1:-1, :-2]
    northern = extended[:, :, 2:, 1:-1]
    southern = extended[:, :, :-2, 1:-1]
    latitude = (row_index.astype(jnp.float32) + 0.5) * (math.pi / total_rows) - 0.5 * math.pi
    metric = (1.0 / jnp.maximum(jnp.cos(latitude), FLOOR))[:, None]
    coriolis = jnp.sin(latitude)[:, None]
    zonal_wind = center[0]
    meridional = center[1]
    stepped = center - ADVECT * (zonal_wind * metric * (eastern - western) + meridional * (northern - southern))
    stepped = stepped + DIFFUSE * (eastern + western + northern + southern - 4.0 * center)
    zonal_new = stepped[0] + ROTATE * coriolis * meridional
    meridional_new = stepped[1] - ROTATE * coriolis * zonal_wind
    return jnp.concatenate([zonal_new[None], meridional_new[None], stepped[2:]], axis=0)


def mix_columns(column_fields, column_mix):
    levels = column_fields.shape[1]
    level_ids = jnp.arange(levels)
    at_end = jnp.where((level_ids == 0) | (level_ids == levels - 1), 1.0, 0.0).astype(column_fields.dtype)
    by_level = jnp.moveaxis(column_fields, 1, 0)

    def forward(carry, inputs):
        upper_ratio, upper_value = carry
        level_value, end_flag = inputs
        diagonal = 1.0 + (2.0 - end_flag) * column_mix
        denominator = diagonal + column_mix * upper_ratio
        ratio = -column_mix / denominator
        value = (level_value + column_mix * upper_value) / denominator
        return (ratio, value), (ratio, value)

    start = (jnp.zeros_like(column_mix), jnp.zeros_like(by_level[0]))
    unused, (ratios, values) = lax.scan(forward, start, (by_level, at_end))

    def backward(below, inputs):
        ratio, value = inputs
        solved = value - ratio * below
        return solved, solved

    unused_last, solved = lax.scan(backward, jnp.zeros_like(by_level[0]), (ratios, values), reverse=True)
    return jnp.moveaxis(solved, 0, 1)


def physics(column_fields, column_mix, column_sun):
    solved = mix_columns(column_fields, column_mix)
    warmed = solved[2] + RADIATE * column_sun * solved[3]
    heating = warmed - column_fields[2]
    return jnp.stack([solved[0], solved[1], warmed, solved[3]]), heating


def reference(state, mixing, insolation, filter_rows, block_map):
    fields, levels, total_rows, total_cols = state.shape
    row_index = jnp.arange(total_rows)
    current = state
    for round_index in range(STEPS):
        beside_all = jnp.concatenate([current[..., -1:], current, current[..., :1]], axis=3)
        beside_all = jnp.pad(beside_all, ((0, 0), (0, 0), (1, 1), (0, 0)))
        stepped = advance(beside_all, row_index, total_rows)
        spectrum = jnp.fft.rfft(stepped, axis=3)
        keep_mask = jnp.arange(spectrum.shape[3]) < KEEP
        spectrum = jnp.where(keep_mask, spectrum, jnp.zeros_like(spectrum))
        smooth = jnp.fft.irfft(spectrum, n=total_cols, axis=3).astype(stepped.dtype)
        current = jnp.where(filter_rows[None, None, :, None] == 1, smooth, stepped)
    flattened = current.reshape(fields, levels, total_rows * total_cols)
    mixed_state, heating = physics(flattened, mixing.reshape(-1), insolation.reshape(-1))
    state_out = mixed_state.reshape(state.shape)
    devices = N_LAT * N_LON
    columns = total_rows * total_cols // devices
    block_table = jnp.zeros((levels, devices * columns), heating.dtype).at[:, block_map.reshape(-1)].set(heating)
    block_heating = jnp.transpose(block_table.reshape(levels, devices, columns), (1, 0, 2))
    return state_out, block_heating
```

```python
import functools
import math

import jax
import jax.numpy as jnp
import numpy as np
from jax import lax
from jax.experimental import pallas as pl
from jax.experimental.pallas import tpu as pltpu
from jax.sharding import PartitionSpec as P

STEPS = 2
KEEP = 64
ADVECT = 0.1
DIFFUSE = 0.1
ROTATE = 0.2
RADIATE = 0.5
FLOOR = 0.25
MESH = pl.DeviceIdType.MESH
F32 = jnp.float32
BF16 = jnp.bfloat16


def filter_tables(fields, tile, n_lon, rank):
    total = tile * n_lon
    ids, waves = np.arange(tile), np.arange(KEEP)
    phase = 2 * np.pi * np.outer(ids, waves) / total
    basis = np.concatenate([np.cos(phase), np.sin(phase[:, 1:])], axis=1)
    basis = basis * np.sqrt(2 / total)
    basis[:, 0] /= np.sqrt(2)
    left = np.linalg.svd(basis, full_matrices=False)[0][:, :rank]
    between = np.zeros((n_lon, rank, n_lon, rank))
    for apart in range(-n_lon + 1, n_lon):
        gap = apart * tile + ids[:, None] - ids[None, :]
        kernel = np.ones(gap.shape) / total
        for wave in range(1, KEEP):
            kernel += (2 / total) * np.cos(2 * np.pi * ((wave * gap) % total) / total)
        block = left.T @ kernel @ left
        for source in range(n_lon):
            if 0 <= source + apart < n_lon:
                between[source, :, source + apart, :] = block.T
    lanes = fields * rank
    analysis = np.zeros((fields, tile, lanes))
    synthesis = np.zeros((lanes, fields, tile))
    for f in range(fields):
        analysis[f, :, f * rank : (f + 1) * rank] = left
        synthesis[f * rank : (f + 1) * rank, f, :] = left.T
    return (
        analysis.reshape(fields * tile, lanes).astype(np.float32),
        between.reshape(n_lon * rank, n_lon * rank).astype(np.float32),
        synthesis.reshape(lanes, fields * tile).astype(np.float32),
    )


def dot(a, b):
    return jnp.dot(a, b, precision=lax.Precision.HIGHEST, preferred_element_type=F32)


def dot_nt(a, b):
    return lax.dot_general(a, b, (((1,), (1,)), ((), ())), preferred_element_type=F32)


def split3(x):
    high = x.astype(BF16)
    rest = x - high.astype(F32)
    middle = rest.astype(BF16)
    low = (rest - middle.astype(F32)).astype(BF16)
    return high, middle, low


def kernel(
    n_lat,
    n_lon,
    state,
    mixing,
    sun,
    wanted_rows,
    block_map,
    analysis,
    between,
    synthesis,
    geometry,
    out,
    block_out,
    stepped,
    current,
    ratios,
    inverses,
    heat,
    lat_send,
    lat_recv,
    lon_send,
    lon_recv,
    z_send,
    z_recv,
    y_send,
    y_recv,
    slot_send,
    slot_recv,
    to_sorted,
    to_slots,
    heat_split,
    heat_send,
    heat_recv,
    halo_ssem,
    halo_rsem,
    z_ssem,
    z_rsem,
    y_ssem,
    y_rsem,
    slot_ssem,
    slot_rsem,
    heat_ssem,
    heat_rsem,
):
    fields, levels, rows, tile = state.shape
    n = n_lat * n_lon
    columns = rows * tile
    per_peer = columns // n
    rank = tile // fields
    share = levels // n_lon
    group = tile // fields
    groups = lon_send.shape[2]
    lat = lax.axis_index("lat")
    lon = lax.axis_index("lon")
    me = lat * n_lon + lon
    east = lax.rem(lon + 1, n_lon)
    west = lax.rem(lon + n_lon - 1, n_lon)

    barrier = pltpu.get_barrier_semaphore()

    @pl.loop(1, n)
    def _(d):
        peer = lax.rem(me + d, n)
        pl.semaphore_signal(
            barrier, inc=1, device_id=(peer // n_lon, lax.rem(peer, n_lon)), device_id_type=MESH
        )

    lane = lax.broadcasted_iota(jnp.int32, (rows, tile), 1)
    row = lax.broadcasted_iota(jnp.int32, (rows, tile), 0)
    metric = geometry[lat, 0]
    coriolis = geometry[lat, 1]
    wanted = jnp.zeros((rows, tile), jnp.int32)
    for r in range(rows):
        wanted = jnp.where(row == r, wanted_rows[lat * rows + r], wanted)
    filtered = (wanted == 1)[None]
    lon_part = lane // rank

    def halo(t, side):
        if side < 2:
            src, dst = lat_send.at[t, side], lat_recv.at[t, side]
            peer = (lat + (1 if side == 0 else -1), lon)
        else:
            src, dst = lon_send.at[t, side - 2], lon_recv.at[t, side - 2]
            peer = (lat, east if side == 2 else west)
        return pltpu.make_async_remote_copy(
            src_ref=src,
            dst_ref=dst,
            send_sem=halo_ssem.at[t, side],
            recv_sem=halo_rsem.at[t, side],
            device_id=peer,
            device_id_type=MESH,
        )

    def pack(t, src):
        for f in range(fields):
            lat_send[t, 0, f] = src[f, :, rows - 1, :]
            lat_send[t, 1, f] = src[f, :, 0, :]
        for g in range(groups):
            lon_send[t, 0, g] = jnp.zeros((rows, tile), F32)
            lon_send[t, 1, g] = jnp.zeros((rows, tile), F32)

        @pl.loop(0, levels)
        def _(l):
            g = l // group
            first = lon_send[t, 1, g]
            last = lon_send[t, 0, g]
            for f in range(fields):
                x = src[f, l]
                spot = lane == lax.rem(l, group) * fields + f
                first = jnp.where(spot, jnp.broadcast_to(x[:, :1], x.shape), first)
                last = jnp.where(spot, jnp.broadcast_to(x[:, tile - 1 :], x.shape), last)
            lon_send[t, 1, g] = first
            lon_send[t, 0, g] = last

    def start_halos(t):
        halo(t, 2).start()
        halo(t, 3).start()

        @pl.when(lat < n_lat - 1)
        def _():
            halo(t, 0).start()

        @pl.when(lat > 0)
        def _():
            halo(t, 1).start()

    def wait_halos(t):
        @pl.when(lat > 0)
        def _():
            halo(t, 0).wait_recv()

        @pl.when(lat == 0)
        def _():
            lat_recv[t, 0] = jnp.zeros(lat_recv.shape[2:], F32)

        @pl.when(lat < n_lat - 1)
        def _():
            halo(t, 1).wait_recv()

        @pl.when(lat == n_lat - 1)
        def _():
            lat_recv[t, 1] = jnp.zeros(lat_recv.shape[2:], F32)

        halo(t, 2).wait_recv()
        halo(t, 3).wait_recv()

    def wait_halo_sends(t):
        @pl.when(lat < n_lat - 1)
        def _():
            halo(t, 0).wait_send()

        @pl.when(lat > 0)
        def _():
            halo(t, 1).wait_send()

        halo(t, 2).wait_send()
        halo(t, 3).wait_send()

    def advance(t, src):
        @pl.loop(0, levels)
        def _(l):
            g = l // group
            from_west = lon_recv[t, 0, g]
            from_east = lon_recv[t, 1, g]
            u = src[0, l]
            v = src[1, l]
            zonal = u * metric
            for f in range(fields):
                x = src[f, l]
                spot = lax.rem(l, group) * fields + f
                eastern = jnp.where(
                    lane == tile - 1,
                    pltpu.roll(from_east, tile - 1 - spot, 1),
                    pltpu.roll(x, tile - 1, 1),
                )
                western = jnp.where(
                    lane == 0,
                    pltpu.roll(from_west, lax.rem(tile - spot, tile), 1),
                    pltpu.roll(x, 1, 1),
                )
                northern = jnp.where(
                    row == rows - 1, lat_recv[t, 1, f, pl.ds(l, 1), :], pltpu.roll(x, rows - 1, 0)
                )
                southern = jnp.where(row == 0, lat_recv[t, 0, f, pl.ds(l, 1), :], pltpu.roll(x, 1, 0))
                new = x - ADVECT * (zonal * (eastern - western) + v * (northern - southern))
                new = new + DIFFUSE * (eastern + western + northern + southern - 4.0 * x)
                if f == 0:
                    new = new + ROTATE * coriolis * v
                if f == 1:
                    new = new - ROTATE * coriolis * u
                stepped[f, l] = new

    def z_copy(t, d):
        owner = lax.rem(lon + d, n_lon)
        return pltpu.make_async_remote_copy(
            src_ref=z_send.at[t, d],
            dst_ref=z_recv.at[t, d],
            send_sem=z_ssem.at[t, d],
            recv_sem=z_rsem.at[t, d],
            device_id=(lat, owner),
            device_id_type=MESH,
        )

    def y_copy(t, d):
        source = lax.rem(lon + n_lon - d, n_lon)
        return pltpu.make_async_remote_copy(
            src_ref=y_send.at[t, d],
            dst_ref=y_recv.at[t, d],
            send_sem=y_ssem.at[t, d],
            recv_sem=y_rsem.at[t, d],
            device_id=(lat, source),
            device_id_type=MESH,
        )

    def analyse(t):
        @pl.loop(1, n_lon + 1)
        def _(step):
            d = lax.rem(step, n_lon)
            start = lax.rem(lon + d, n_lon) * share
            parts = [
                stepped[f, pl.ds(start, share)].reshape(share * rows, tile) for f in range(fields)
            ]
            z = dot(jnp.concatenate(parts, axis=1), analysis[...])

            @pl.when(d > 0)
            def _():
                z_send[t, d] = z.reshape(share, rows, tile)
                z_copy(t, d).start()

            @pl.when(d == 0)
            def _():
                z_recv[t, 0] = z.reshape(share, rows, tile)

    def own(t):
        @pl.loop(1, n_lon)
        def _(d):
            z_copy(t, d).wait_recv()

        count = share * rows
        wide = lax.broadcasted_iota(jnp.int32, (count, tile), 1) // rank
        halves = []
        for h in range(n_lon // fields):
            got = []
            for k in range(fields):
                d = lax.rem(lon + n_lon - (h * fields + k), n_lon)
                got.append(z_recv[t, d].reshape(count, tile))
            per_field = []
            for f in range(fields):
                total = got[0] if f == 0 else pltpu.roll(got[0], tile - rank * f, 1)
                for k in range(1, fields):
                    shift = (rank * (k - f)) % tile
                    moved = pltpu.roll(got[k], shift, 1) if shift else got[k]
                    total = jnp.where(wide == k, moved, total)
                per_field.append(total)
            halves.append(jnp.concatenate(per_field, axis=0))
        y = dot(jnp.concatenate(halves, axis=1), between[...])
        for p in range(n_lon):
            h, k = p // fields, p % fields
            total = None
            for f in range(fields):
                piece = y[f * count : (f + 1) * count, h * tile : (h + 1) * tile]
                shift = (rank * (f - k)) % tile
                piece = pltpu.roll(piece, shift, 1) if shift else piece
                total = piece if total is None else jnp.where(wide == f, piece, total)
            d = lax.rem(lon + n_lon - p, n_lon)
            total = total.reshape(share, rows, tile)

            @pl.when(d > 0)
            def _():
                y_send[t, d] = total
                y_copy(t, d).start()

            @pl.when(d == 0)
            def _():
                y_recv[t, 0] = total

    def synthesise(t):
        @pl.loop(0, n_lon)
        def _(d):
            @pl.when(d > 0)
            def _():
                y_copy(t, d).wait_recv()

            start = lax.rem(lon + d, n_lon) * share
            smooth = dot(y_recv[t, d].reshape(share * rows, tile), synthesis[...])
            for f in range(fields):
                piece = smooth[:, f * tile : (f + 1) * tile].reshape(share, rows, tile)
                here = pl.ds(start, share)
                current[f, here] = jnp.where(filtered, piece, stepped[f, here])

    def slot_copy(d):
        peer = lax.rem(me + d, n)
        return pltpu.make_async_remote_copy(
            src_ref=slot_send.at[peer],
            dst_ref=slot_recv.at[me],
            send_sem=slot_ssem.at[d],
            recv_sem=slot_rsem.at[d],
            device_id=(peer // n_lon, lax.rem(peer, n_lon)),
            device_id_type=MESH,
        )

    def heat_copy(d):
        peer = lax.rem(me + d, n)
        there = pl.ds(pl.multiple_of(peer * per_peer, per_peer), per_peer)
        here = pl.ds(pl.multiple_of(me * per_peer, per_peer), per_peer)
        return pltpu.make_async_remote_copy(
            src_ref=heat_send.at[there],
            dst_ref=heat_recv.at[here],
            send_sem=heat_ssem.at[d],
            recv_sem=heat_rsem.at[d],
            device_id=(peer // n_lon, lax.rem(peer, n_lon)),
            device_id_type=MESH,
        )

    def sort_columns():
        mapped = block_map[...].astype(F32)
        target = jnp.floor((mapped + 0.5) * (1.0 / columns))
        slot = mapped - target * columns
        slot_high = slot.astype(BF16)
        slot_low = (slot - slot_high.astype(F32)).astype(BF16)
        peers = lax.broadcasted_iota(jnp.int32, (n, tile), 0).astype(F32)
        before = lax.broadcasted_iota(jnp.int32, (tile, tile), 0)
        after = lax.broadcasted_iota(jnp.int32, (tile, tile), 1)
        earlier = (before < after).astype(F32).astype(BF16)
        positions = lax.broadcasted_iota(jnp.int32, (columns, tile), 0).astype(F32)
        places = lax.broadcasted_iota(jnp.int32, (tile, tile), 0).astype(F32)
        base = jnp.zeros((n, 1), F32)
        slots = jnp.zeros((n, tile), F32)
        for r in range(rows):
            hit = (peers == target[r : r + 1]).astype(F32)
            prefix = jnp.dot(hit.astype(BF16), earlier, preferred_element_type=F32) + base
            base = base + jnp.sum(hit, axis=1, keepdims=True)
            order = jnp.sum(hit * prefix, axis=0, keepdims=True)
            spot = target[r : r + 1] * per_peer + order
            to_sorted[:, r * tile : (r + 1) * tile] = (positions == spot).astype(F32).astype(BF16)
            named = (places == order).astype(F32)
            for part in (slot_high, slot_low):
                weighted = (named * part[r : r + 1].astype(F32)).astype(BF16)
                slots = slots + dot_nt(hit.astype(BF16), weighted)
        slot_send[...] = jnp.broadcast_to(slots[:, None, :], slot_send.shape)
        slot_recv[me] = slot_send[me]

        @pl.loop(1, n)
        def _(d):
            slot_copy(d).start()

    def place_columns():
        @pl.loop(1, n)
        def _(d):
            slot_copy(d).wait_recv()

        names = slot_recv[:, 0, :].T
        ids = lax.broadcasted_iota(jnp.int32, (per_peer, columns), 1).astype(F32)
        for source in range(n):
            column = names[:per_peer, source : source + 1]
            to_slots[source * per_peer : (source + 1) * per_peer, :] = (ids == column).astype(F32)

    def ratios_of_levels():
        mix = mixing[...]

        def body(l, upper):
            at_end = jnp.logical_or(l == 0, l == levels - 1)
            diagonal = 1.0 + jnp.where(at_end, 1.0, 2.0) * mix
            inverse = 1.0 / (diagonal + mix * upper)
            ratio = -mix * inverse
            inverses[l] = inverse
            ratios[l] = ratio
            return ratio

        lax.fori_loop(0, levels, body, jnp.zeros((rows, tile), F32))

    def mix_levels():
        mix = mixing[...]

        def forward(l, above):
            inverse = inverses[l]
            values = tuple((current[f, l] + mix * above[f]) * inverse for f in range(fields))
            for f in range(fields):
                out[f, l] = values[f]
            return values

        zeros = tuple(jnp.zeros((rows, tile), F32) for f in range(fields))
        lax.fori_loop(0, levels, forward, zeros, unroll=4)
        warming = RADIATE * sun[...]

        def backward(step, below):
            l = levels - 1 - step
            ratio = ratios[l]
            solved = tuple(out[f, l] - ratio * below[f] for f in range(fields))
            for f in range(fields):
                if f == 2:
                    warmed = solved[2] + warming * solved[3]
                    out[2, l] = warmed
                    heat[l] = warmed - current[2, l]
                else:
                    out[f, l] = solved[f]
            return solved

        lax.fori_loop(0, levels, backward, zeros, unroll=4)

    def send_heat():
        for r in range(rows):
            for k, part in enumerate(split3(heat[:, r, :])):
                heat_split[k, :levels, r * tile : (r + 1) * tile] = part
                if levels < tile:
                    heat_split[k, levels:, r * tile : (r + 1) * tile] = jnp.zeros(
                        (tile - levels, tile), BF16
                    )
        table = heat_split[...].reshape(3 * tile, columns)
        sorted3 = dot_nt(to_sorted[...], table)
        heat_send[...] = sorted3[:, :tile] + sorted3[:, tile : 2 * tile] + sorted3[:, 2 * tile :]

        @pl.loop(1, n)
        def _(d):
            heat_copy(d).start()

        mine = pl.ds(pl.multiple_of(me * per_peer, per_peer), per_peer)
        heat_recv[mine] = heat_send[mine]

    def place_heat():
        @pl.loop(1, n)
        def _(d):
            heat_copy(d).wait_recv()

        table = jnp.concatenate(split3(heat_recv[...].T), axis=0)
        placed = jnp.dot(table, to_slots[...].astype(BF16), preferred_element_type=F32)
        total = placed[:tile] + placed[tile : 2 * tile] + placed[2 * tile :]
        block_out[0] = total[:levels]

    pack(0, state)
    pl.semaphore_wait(barrier, n - 1)
    start_halos(0)
    sort_columns()
    wait_halos(0)
    advance(0, state)
    analyse(0)
    ratios_of_levels()
    own(0)
    place_columns()
    synthesise(0)
    for t in range(1, STEPS):
        pack(t, current)
        start_halos(t)
        wait_halos(t)
        advance(t, current)
        analyse(t)
        own(t)
        synthesise(t)
    mix_levels()
    send_heat()
    place_heat()

    for t in range(STEPS):
        wait_halo_sends(t)

        @pl.loop(1, n_lon)
        def _(d):
            z_copy(t, d).wait_send()
            y_copy(t, d).wait_send()

    @pl.loop(1, n)
    def _(d):
        slot_copy(d).wait_send()
        heat_copy(d).wait_send()


def per_device(n_lat, n_lon, state, mixing, insolation, filter_rows, block_map):
    fields, levels, rows, tile = state.shape
    n = n_lat * n_lon
    columns = rows * tile
    per_peer = columns // n
    rank = tile // fields
    share = levels // n_lon
    groups = -(-levels * fields // tile)
    analysis, between, synthesis = filter_tables(fields, tile, n_lon, rank)
    total_rows = rows * n_lat
    latitude = (np.arange(total_rows) + 0.5) * (math.pi / total_rows) - 0.5 * math.pi
    by_row = np.stack([1.0 / np.maximum(np.cos(latitude), FLOOR), np.sin(latitude)])
    by_row = by_row.reshape(2, n_lat, rows, 1).transpose(1, 0, 2, 3)
    geometry = np.broadcast_to(by_row, (n_lat, 2, rows, tile)).astype(np.float32)
    vmem = pl.BlockSpec(memory_space=pltpu.VMEM)
    smem = pl.BlockSpec(memory_space=pltpu.SMEM)
    block = (share, rows, tile)
    sems = pltpu.SemaphoreType.DMA
    return pl.pallas_call(
        functools.partial(kernel, n_lat, n_lon),
        out_shape=(
            jax.ShapeDtypeStruct(state.shape, F32),
            jax.ShapeDtypeStruct((1, levels, columns), F32),
        ),
        in_specs=[vmem, vmem, vmem, smem, vmem, vmem, vmem, vmem, vmem],
        out_specs=(vmem, vmem),
        scratch_shapes=[
            pltpu.VMEM(state.shape, F32),
            pltpu.VMEM(state.shape, F32),
            pltpu.VMEM((levels, rows, tile), F32),
            pltpu.VMEM((levels, rows, tile), F32),
            pltpu.VMEM((levels, rows, tile), F32),
            pltpu.VMEM((STEPS, 2, fields, levels, tile), F32),
            pltpu.VMEM((STEPS, 2, fields, levels, tile), F32),
            pltpu.VMEM((STEPS, 2, groups, rows, tile), F32),
            pltpu.VMEM((STEPS, 2, groups, rows, tile), F32),
            pltpu.VMEM((STEPS, n_lon) + block, F32),
            pltpu.VMEM((STEPS, n_lon) + block, F32),
            pltpu.VMEM((STEPS, n_lon) + block, F32),
            pltpu.VMEM((STEPS, n_lon) + block, F32),
            pltpu.VMEM((n, 8, tile), F32),
            pltpu.VMEM((n, 8, tile), F32),
            pltpu.VMEM((columns, columns), BF16),
            pltpu.VMEM((columns, columns), F32),
            pltpu.VMEM((3, tile, columns), BF16),
            pltpu.VMEM((columns, tile), F32),
            pltpu.VMEM((columns, tile), F32),
            sems((STEPS, 4)),
            sems((STEPS, 4)),
            sems((STEPS, n_lon)),
            sems((STEPS, n_lon)),
            sems((STEPS, n_lon)),
            sems((STEPS, n_lon)),
            sems((n,)),
            sems((n,)),
            sems((n,)),
            sems((n,)),
        ],
        compiler_params=pltpu.CompilerParams(
            collective_id=0, has_side_effects=True, vmem_limit_bytes=48 * 1024 * 1024
        ),
        cost_estimate=pl.CostEstimate(flops=8 * 10**9, bytes_accessed=6 * 10**6, transcendentals=0),
    )(state, mixing, insolation, filter_rows, block_map, analysis, between, synthesis, geometry)


def solution(mesh):
    n_lat, n_lon = mesh.shape["lat"], mesh.shape["lon"]
    in_specs = (P(None, None, "lat", "lon"), P("lat", "lon"), P("lat", "lon"), P(), P("lat", "lon"))
    out_specs = (P(None, None, "lat", "lon"), P(("lat", "lon"), None, None))
    return jax.shard_map(
        functools.partial(per_device, n_lat, n_lon),
        mesh=mesh,
        in_specs=in_specs,
        out_specs=out_specs,
        check_vma=False,
    )
```

```python
import functools
import math

import jax
import jax.numpy as jnp
import ml_dtypes
import numpy as np
from jax import lax
from jax.experimental import pallas as pl
from jax.experimental.pallas import tpu as pltpu
from jax.sharding import PartitionSpec as P

STEPS = 2
KEEP = 64
ADVECT = 0.1
DIFFUSE = 0.1
ROTATE = 0.2
RADIATE = 0.5
FLOOR = 0.25
MESH = pl.DeviceIdType.MESH
F32 = jnp.float32
BF16 = jnp.bfloat16


def filter_tables(fields, tile, n_lon, rank):
    total = tile * n_lon
    ids, waves = np.arange(tile), np.arange(KEEP)
    phase = 2 * np.pi * np.outer(ids, waves) / total
    basis = np.concatenate([np.cos(phase), np.sin(phase[:, 1:])], axis=1)
    basis = basis * np.sqrt(2 / total)
    basis[:, 0] /= np.sqrt(2)
    left = np.linalg.svd(basis, full_matrices=False)[0][:, :rank]
    between = np.zeros((n_lon, rank, n_lon, rank))
    for apart in range(-n_lon + 1, n_lon):
        gap = apart * tile + ids[:, None] - ids[None, :]
        kernel = np.ones(gap.shape) / total
        for wave in range(1, KEEP):
            kernel += (2 / total) * np.cos(2 * np.pi * ((wave * gap) % total) / total)
        block = left.T @ kernel @ left
        for source in range(n_lon):
            if 0 <= source + apart < n_lon:
                between[source, :, source + apart, :] = block.T
    lanes = fields * rank
    analysis = np.zeros((fields, tile, lanes))
    synthesis = np.zeros((lanes, fields, tile))
    for f in range(fields):
        analysis[f, :, f * rank : (f + 1) * rank] = left
        synthesis[f * rank : (f + 1) * rank, f, :] = left.T
    analysis = parts_of(analysis.reshape(fields * tile, lanes))
    between = parts_of(between.reshape(n_lon * rank, n_lon * rank))
    high, low = parts_of(synthesis.reshape(lanes, fields * tile))
    return (
        np.concatenate(analysis, axis=1),
        np.concatenate(between, axis=1),
        np.concatenate([high, high, low], axis=0),
    )


def parts_of(table):
    high = table.astype(ml_dtypes.bfloat16)
    return high, (table - high.astype(np.float64)).astype(ml_dtypes.bfloat16)


def split2(x):
    high = x.astype(BF16)
    return high, (x - high.astype(F32)).astype(BF16)


def dot(a, b):
    return jnp.dot(a, b, preferred_element_type=F32)


def dot_parts(x, table):
    width = table.shape[1] // 2
    high, low = split2(x)
    both = dot(high, table[...])
    return both[:, :width] + both[:, width:] + dot(low, table[:, :width])


def dot_nt(a, b):
    return lax.dot_general(a, b, (((1,), (1,)), ((), ())), preferred_element_type=F32)


def split3(x):
    high = x.astype(BF16)
    rest = x - high.astype(F32)
    middle = rest.astype(BF16)
    low = (rest - middle.astype(F32)).astype(BF16)
    return high, middle, low


def kernel(
    n_lat,
    n_lon,
    batches,
    state_in,
    mixing_in,
    sun_in,
    rows_in,
    map_in,
    analysis_in,
    between_in,
    synthesis_in,
    geometry_in,
    out,
    block_out,
    state,
    mixing,
    sun,
    wanted_rows,
    block_map,
    analysis,
    between,
    synthesis,
    geometry,
    in_sem,
    stepped,
    current,
    ratios,
    inverses,
    heat,
    to_sorted,
    to_slots,
    heat_split,
    heat_send,
    heat_recv,
    slot_send,
    slot_recv,
    slot_ssem,
    slot_rsem,
    heat_ssem,
    heat_rsem,
    *batch_refs,
):
    fields, levels, rows, tile = state.shape
    n = n_lat * n_lon
    columns = rows * tile
    per_peer = columns // n
    rank = tile // fields
    group = tile // fields
    wire = heat_send.shape[0] // n
    lat = lax.axis_index("lat")
    lon = lax.axis_index("lon")
    me = lat * n_lon + lon
    east = lax.rem(lon + 1, n_lon)
    west = lax.rem(lon + n_lon - 1, n_lon)

    sources = (
        state_in,
        mixing_in,
        sun_in,
        rows_in,
        map_in,
        analysis_in,
        between_in,
        synthesis_in,
        geometry_in,
    )
    places = (state, mixing, sun, wanted_rows, block_map, analysis, between, synthesis, geometry)
    loads = [
        pltpu.make_async_copy(src, dst, in_sem.at[k])
        for k, (src, dst) in enumerate(zip(sources, places))
    ]
    for load in loads:
        load.start()

    barrier = pltpu.get_barrier_semaphore()

    @pl.loop(1, n)
    def _(d):
        peer = lax.rem(me + d, n)
        pl.semaphore_signal(
            barrier, inc=1, device_id=(peer // n_lon, lax.rem(peer, n_lon)), device_id_type=MESH
        )

    lane = lax.broadcasted_iota(jnp.int32, (rows, tile), 1)
    row = lax.broadcasted_iota(jnp.int32, (rows, tile), 0)

    class Batch:
        pass

    def make_batch(b):
        first, share = batches[b]
        count = share * n_lon
        (
            lat_send,
            lat_recv,
            lon_send,
            lon_recv,
            z_send,
            z_recv,
            y_send,
            y_recv,
            halo_ssem,
            halo_rsem,
            z_ssem,
            z_rsem,
            y_ssem,
            y_rsem,
        ) = batch_refs[b * 14 : (b + 1) * 14]
        groups = lon_send.shape[2]
        here = pl.ds(first, count)
        many = share * rows

        def halo(t, side):
            if side < 2:
                src, dst = lat_send.at[t, side], lat_recv.at[t, side]
                peer = (lat + (1 if side == 0 else -1), lon)
            else:
                src, dst = lon_send.at[t, side - 2], lon_recv.at[t, side - 2]
                peer = (lat, east if side == 2 else west)
            return pltpu.make_async_remote_copy(
                src_ref=src,
                dst_ref=dst,
                send_sem=halo_ssem.at[t, side],
                recv_sem=halo_rsem.at[t, side],
                device_id=peer,
                device_id_type=MESH,
            )

        def pack(t, src):
            for f in range(fields):
                lat_send[t, 0, f] = src[f, here, rows - 1, :]
                lat_send[t, 1, f] = src[f, here, 0, :]
            for g in range(groups):
                lon_send[t, 0, g] = jnp.zeros((rows, tile), F32)
                lon_send[t, 1, g] = jnp.zeros((rows, tile), F32)
            chunk = math.gcd(math.gcd(count, group), 8)

            @pl.loop(0, count // chunk)
            def _(c):
                g = c * chunk // group
                low = lon_send[t, 1, g]
                high = lon_send[t, 0, g]
                for k in range(chunk):
                    l = c * chunk + k
                    for f in range(fields):
                        x = src[f, first + l]
                        spot = lane == lax.rem(l, group) * fields + f
                        low = jnp.where(spot, jnp.broadcast_to(x[:, :1], x.shape), low)
                        high = jnp.where(spot, jnp.broadcast_to(x[:, tile - 1 :], x.shape), high)
                lon_send[t, 1, g] = low
                lon_send[t, 0, g] = high

        def start_halos(t):
            halo(t, 2).start()
            halo(t, 3).start()

            @pl.when(lat < n_lat - 1)
            def _():
                halo(t, 0).start()

            @pl.when(lat > 0)
            def _():
                halo(t, 1).start()

        def wait_halos(t):
            @pl.when(lat > 0)
            def _():
                halo(t, 0).wait_recv()

            @pl.when(lat == 0)
            def _():
                lat_recv[t, 0] = jnp.zeros(lat_recv.shape[2:], F32)

            @pl.when(lat < n_lat - 1)
            def _():
                halo(t, 1).wait_recv()

            @pl.when(lat == n_lat - 1)
            def _():
                lat_recv[t, 1] = jnp.zeros(lat_recv.shape[2:], F32)

            halo(t, 2).wait_recv()
            halo(t, 3).wait_recv()

        def wait_halo_sends(t):
            @pl.when(lat < n_lat - 1)
            def _():
                halo(t, 0).wait_send()

            @pl.when(lat > 0)
            def _():
                halo(t, 1).wait_send()

            halo(t, 2).wait_send()
            halo(t, 3).wait_send()

        def advance(t, src):
            metric = geometry[lat, 0]
            coriolis = geometry[lat, 1]

            def one(l):
                g = l // group
                from_west = lon_recv[t, 0, g]
                from_east = lon_recv[t, 1, g]
                u = src[0, first + l]
                v = src[1, first + l]
                zonal = u * metric
                made = []
                for f in range(fields):
                    x = src[f, first + l]
                    spot = lax.rem(l, group) * fields + f
                    eastern = jnp.where(
                        lane == tile - 1,
                        pltpu.roll(from_east, tile - 1 - spot, 1),
                        pltpu.roll(x, tile - 1, 1),
                    )
                    western = jnp.where(
                        lane == 0,
                        pltpu.roll(from_west, lax.rem(tile - spot, tile), 1),
                        pltpu.roll(x, 1, 1),
                    )
                    northern = jnp.where(
                        row == rows - 1,
                        lat_recv[t, 1, f, pl.ds(l, 1), :],
                        pltpu.roll(x, rows - 1, 0),
                    )
                    southern = jnp.where(
                        row == 0, lat_recv[t, 0, f, pl.ds(l, 1), :], pltpu.roll(x, 1, 0)
                    )
                    new = x - ADVECT * (zonal * (eastern - western) + v * (northern - southern))
                    new = new + DIFFUSE * (eastern + western + northern + southern - 4.0 * x)
                    if f == 0:
                        new = new + ROTATE * coriolis * v
                    if f == 1:
                        new = new - ROTATE * coriolis * u
                    made.append(new)
                return made

            chunk = math.gcd(count, 4)

            @pl.loop(0, count // chunk)
            def _(c):
                made = [one(c * chunk + k) for k in range(chunk)]
                for k in range(chunk):
                    for f in range(fields):
                        stepped[f, first + c * chunk + k] = made[k][f]

        def z_copy(t, d):
            owner = lax.rem(lon + d, n_lon)
            return pltpu.make_async_remote_copy(
                src_ref=z_send.at[t, owner],
                dst_ref=z_recv.at[t, lon],
                send_sem=z_ssem.at[t, d],
                recv_sem=z_rsem.at[t, d],
                device_id=(lat, owner),
                device_id_type=MESH,
            )

        def y_copy(t, d):
            source = lax.rem(lon + d, n_lon)
            return pltpu.make_async_remote_copy(
                src_ref=y_send.at[t, source],
                dst_ref=y_recv.at[t, lon],
                send_sem=y_ssem.at[t, d],
                recv_sem=y_rsem.at[t, d],
                device_id=(lat, source),
                device_id_type=MESH,
            )

        def analyse(t):
            parts = [stepped[f, here].reshape(count * rows, tile) for f in range(fields)]
            z = dot_parts(jnp.concatenate(parts, axis=1), analysis)
            z_send[t] = z.reshape(n_lon, share, rows, tile)

            @pl.loop(1, n_lon)
            def _(d):
                z_copy(t, d).start()

            z_recv[t, lon] = z_send[t, lon]

        def own(t):
            @pl.loop(1, n_lon)
            def _(d):
                z_copy(t, d).wait_recv()

            wide = lax.broadcasted_iota(jnp.int32, (many, tile), 1) // rank
            halves = []
            for h in range(n_lon // fields):
                got = [z_recv[t, h * fields + k].reshape(many, tile) for k in range(fields)]
                per_field = []
                for f in range(fields):
                    total = None
                    for k in range(fields):
                        shift = (rank * (k - f)) % tile
                        moved = pltpu.roll(got[k], shift, 1) if shift else got[k]
                        total = moved if k == 0 else jnp.where(wide == k, moved, total)
                    per_field.append(total)
                halves.append(jnp.concatenate(per_field, axis=0))
            y = dot_parts(jnp.concatenate(halves, axis=1), between)
            for p in range(n_lon):
                h, k = p // fields, p % fields
                total = None
                for f in range(fields):
                    piece = y[f * many : (f + 1) * many, h * tile : (h + 1) * tile]
                    shift = (rank * (f - k)) % tile
                    piece = pltpu.roll(piece, shift, 1) if shift else piece
                    total = piece if f == 0 else jnp.where(wide == f, piece, total)
                y_send[t, p] = total.reshape(share, rows, tile)

            @pl.loop(1, n_lon)
            def _(d):
                y_copy(t, d).start()

            y_recv[t, lon] = y_send[t, lon]

        def synthesise(t):
            wanted = jnp.zeros((rows, tile), jnp.int32)
            for r in range(rows):
                wanted = jnp.where(row == r, wanted_rows[lat * rows + r], wanted)
            filtered = (wanted == 1)[None]

            @pl.loop(1, n_lon)
            def _(d):
                y_copy(t, d).wait_recv()

            high, low = split2(y_recv[t].reshape(count * rows, tile))
            smooth = dot(jnp.concatenate([high, low, high], axis=1), synthesis[...])
            for f in range(fields):
                piece = smooth[:, f * tile : (f + 1) * tile].reshape(count, rows, tile)
                current[f, here] = jnp.where(filtered, piece, stepped[f, here])

        def wait_sends(t):
            wait_halo_sends(t)

            @pl.loop(1, n_lon)
            def _(d):
                z_copy(t, d).wait_send()
                y_copy(t, d).wait_send()

        batch = Batch()
        batch.first, batch.count = first, count
        batch.pack, batch.start_halos, batch.wait_halos = pack, start_halos, wait_halos
        batch.advance, batch.analyse, batch.own = advance, analyse, own
        batch.synthesise, batch.wait_sends = synthesise, wait_sends
        return batch

    def slot_copy(d):
        peer = lax.rem(me + d, n)
        return pltpu.make_async_remote_copy(
            src_ref=slot_send.at[peer],
            dst_ref=slot_recv.at[me],
            send_sem=slot_ssem.at[d],
            recv_sem=slot_rsem.at[d],
            device_id=(peer // n_lon, lax.rem(peer, n_lon)),
            device_id_type=MESH,
        )

    def heat_copy(d):
        peer = lax.rem(me + d, n)
        there = pl.ds(pl.multiple_of(peer * wire, wire), wire)
        here = pl.ds(pl.multiple_of(me * wire, wire), wire)
        return pltpu.make_async_remote_copy(
            src_ref=heat_send.at[there],
            dst_ref=heat_recv.at[here],
            send_sem=heat_ssem.at[d],
            recv_sem=heat_rsem.at[d],
            device_id=(peer // n_lon, lax.rem(peer, n_lon)),
            device_id_type=MESH,
        )

    def sort_columns():
        mapped = block_map[...].astype(F32)
        target = jnp.floor((mapped + 0.5) * (1.0 / columns))
        slot = mapped - target * columns
        slot_high = slot.astype(BF16)
        slot_low = (slot - slot_high.astype(F32)).astype(BF16)
        peers = lax.broadcasted_iota(jnp.int32, (n, tile), 0).astype(F32)
        before = lax.broadcasted_iota(jnp.int32, (tile, tile), 0)
        after = lax.broadcasted_iota(jnp.int32, (tile, tile), 1)
        earlier = (before < after).astype(F32).astype(BF16)
        positions = lax.broadcasted_iota(jnp.int32, (columns, tile), 0).astype(F32)
        places = lax.broadcasted_iota(jnp.int32, (tile, tile), 0).astype(F32)
        base = jnp.zeros((n, 1), F32)
        slots = jnp.zeros((n, tile), F32)
        for r in range(rows):
            hit = (peers == target[r : r + 1]).astype(F32)
            prefix = dot(hit.astype(BF16), earlier) + base
            base = base + jnp.sum(hit, axis=1, keepdims=True)
            order = jnp.sum(hit * prefix, axis=0, keepdims=True)
            spot = target[r : r + 1] * per_peer + order
            to_sorted[:, r * tile : (r + 1) * tile] = (positions == spot).astype(F32).astype(BF16)
            named = (places == order).astype(F32)
            for part in (slot_high, slot_low):
                weighted = (named * part[r : r + 1].astype(F32)).astype(BF16)
                slots = slots + dot_nt(hit.astype(BF16), weighted)
        slot_send[...] = jnp.broadcast_to(slots[:, None, :], slot_send.shape)
        slot_recv[me] = slot_send[me]

        @pl.loop(1, n)
        def _(d):
            slot_copy(d).start()

    def place_columns():
        @pl.loop(1, n)
        def _(d):
            slot_copy(d).wait_recv()

        names = slot_recv[:, 0, :].T[:per_peer]
        join = max(1, 16 // per_peer)
        size = join * per_peer
        ids = lax.broadcasted_iota(jnp.int32, (size, columns), 1).astype(F32)
        for k in range(n // join):
            picked = [names[:, s : s + 1] for s in range(k * join, (k + 1) * join)]
            column = picked[0] if join == 1 else jnp.concatenate(picked, axis=0)
            to_slots[k * size : (k + 1) * size, :] = (ids == column).astype(F32).astype(BF16)

    def ratios_of_levels():
        mix = mixing[...]

        def body(l, upper):
            at_end = jnp.logical_or(l == 0, l == levels - 1)
            diagonal = 1.0 + jnp.where(at_end, 1.0, 2.0) * mix
            inverse = 1.0 / (diagonal + mix * upper)
            ratio = -mix * inverse
            inverses[l] = inverse
            ratios[l] = ratio
            return ratio

        lax.fori_loop(0, levels, body, jnp.zeros((rows, tile), F32))

    zeros = tuple(jnp.zeros((rows, tile), F32) for f in range(fields))

    def mix_down(batch, carried):
        mix = mixing[...]

        def forward(l, above):
            inverse = inverses[l]
            values = tuple((current[f, l] + mix * above[f]) * inverse for f in range(fields))
            for f in range(fields):
                out[f, l] = values[f]
            return values

        return lax.fori_loop(batch.first, batch.first + batch.count, forward, carried, unroll=8)

    def mix_up():
        warming = RADIATE * sun[...]

        def backward(step, below):
            l = levels - 1 - step
            ratio = ratios[l]
            solved = tuple(out[f, l] - ratio * below[f] for f in range(fields))
            for f in range(fields):
                if f == 2:
                    warmed = solved[2] + warming * solved[3]
                    out[2, l] = warmed
                    heat[l] = warmed - current[2, l]
                else:
                    out[f, l] = solved[f]
            return solved

        lax.fori_loop(0, levels, backward, zeros, unroll=8)

    spill = per_peer - wire
    half = levels // 2

    def send_heat():
        for r in range(rows):
            for k, part in enumerate(split3(heat[:, r, :])):
                heat_split[k, :levels, r * tile : (r + 1) * tile] = part
                if levels < tile:
                    heat_split[k, levels:, r * tile : (r + 1) * tile] = jnp.zeros(
                        (tile - levels, tile), BF16
                    )
        table = heat_split[...].reshape(3 * tile, columns)
        sorted3 = dot_nt(to_sorted[...], table)
        sent = sorted3[:, :tile] + sorted3[:, tile : 2 * tile] + sorted3[:, 2 * tile :]
        if spill:
            spots = lax.broadcasted_iota(jnp.int32, (spill, tile), 1)
            free = spots >= levels
            pieces = []
            for p in range(n):
                base = p * per_peer
                extra = sent[base + wire : base + per_peer]
                pieces.append(
                    jnp.where(free, pltpu.roll(extra, levels, 1), sent[base : base + spill])
                )
                pieces.append(
                    jnp.where(
                        free,
                        pltpu.roll(extra, levels - half, 1),
                        sent[base + spill : base + 2 * spill],
                    )
                )
                pieces.append(sent[base + 2 * spill : base + wire])
            sent = jnp.concatenate(pieces, axis=0)
        heat_send[...] = sent

        @pl.loop(1, n)
        def _(d):
            heat_copy(d).start()

        mine = pl.ds(pl.multiple_of(me * wire, wire), wire)
        heat_recv[mine] = heat_send[mine]

    def place_heat():
        @pl.loop(1, n)
        def _(d):
            heat_copy(d).wait_recv()

        got = heat_recv[...]
        if spill:
            spots = lax.broadcasted_iota(jnp.int32, (spill, tile), 1)
            pieces = []
            for p in range(n):
                message = got[p * wire : (p + 1) * wire]
                extra = jnp.where(
                    spots < half,
                    pltpu.roll(message[:spill], tile - levels, 1),
                    pltpu.roll(message[spill : 2 * spill], tile - levels + half, 1),
                )
                pieces += [message, extra]
            got = jnp.concatenate(pieces, axis=0)
        table = jnp.concatenate(split3(got.T), axis=0)
        placed = dot(table, to_slots[...])
        total = placed[:tile] + placed[tile : 2 * tile] + placed[2 * tile :]
        block_out[0] = total[:levels]

    work = [make_batch(b) for b in range(len(batches))]
    loads[0].wait()
    for batch in work:
        batch.pack(0, state)
    pl.semaphore_wait(barrier, n - 1)
    for batch in work:
        batch.start_halos(0)
    for load in loads[1:]:
        load.wait()
    sort_columns()
    for t in range(STEPS):
        source = state if t == 0 else current
        for batch in work:
            batch.wait_halos(t)
            batch.advance(t, source)
            batch.analyse(t)
        if t == 0:
            ratios_of_levels()
        for batch in work:
            batch.own(t)
        if t == 0:
            place_columns()
        carried = zeros
        for batch in work:
            batch.synthesise(t)
            if t + 1 < STEPS:
                batch.pack(t + 1, current)
                batch.start_halos(t + 1)
            else:
                carried = mix_down(batch, carried)
    mix_up()
    send_heat()
    for batch in work:
        for t in range(STEPS):
            batch.wait_sends(t)
    place_heat()

    @pl.loop(1, n)
    def _(d):
        slot_copy(d).wait_send()
        heat_copy(d).wait_send()


def per_device(n_lat, n_lon, state, mixing, insolation, filter_rows, block_map):
    fields, levels, rows, tile = state.shape
    n = n_lat * n_lon
    columns = rows * tile
    per_peer = columns // n
    rank = tile // fields
    share = levels // n_lon
    large = share - share // 2
    batches = ((0, large), (large * n_lon, share - large))
    analysis, between, synthesis = filter_tables(fields, tile, n_lon, rank)
    total_rows = rows * n_lat
    latitude = (np.arange(total_rows) + 0.5) * (math.pi / total_rows) - 0.5 * math.pi
    by_row = np.stack([1.0 / np.maximum(np.cos(latitude), FLOOR), np.sin(latitude)])
    by_row = by_row.reshape(2, n_lat, rows, 1).transpose(1, 0, 2, 3)
    geometry = np.broadcast_to(by_row, (n_lat, 2, rows, tile)).astype(np.float32)
    spare = per_peer % 32 == 0 and levels % 2 == 0 and levels + levels // 2 <= tile
    wire = per_peer * 3 // 4 if spare else per_peer
    vmem = pl.BlockSpec(memory_space=pltpu.VMEM)
    anywhere = pl.BlockSpec(memory_space=pl.ANY)
    sems = pltpu.SemaphoreType.DMA
    operands = (
        state,
        mixing,
        insolation,
        filter_rows,
        block_map,
        analysis,
        between,
        synthesis,
        geometry,
    )
    places = [
        pltpu.SMEM(a.shape, a.dtype) if a is filter_rows else pltpu.VMEM(a.shape, a.dtype)
        for a in operands
    ]
    per_batch = []
    for _, part in batches:
        count = part * n_lon
        edge = (STEPS, 2, fields, count, tile)
        side = (STEPS, 2, -(-count * fields // tile), rows, tile)
        block = (STEPS, n_lon, part, rows, tile)
        for shape in (edge, edge, side, side, block, block, block, block):
            per_batch.append(pltpu.VMEM(shape, F32))
        per_batch += [sems((STEPS, 4))] * 2 + [sems((STEPS, n_lon))] * 4
    return pl.pallas_call(
        functools.partial(kernel, n_lat, n_lon, batches),
        out_shape=(
            jax.ShapeDtypeStruct(state.shape, F32),
            jax.ShapeDtypeStruct((1, levels, columns), F32),
        ),
        in_specs=[anywhere] * len(operands),
        out_specs=(vmem, vmem),
        scratch_shapes=places
        + [
            sems((len(operands),)),
            pltpu.VMEM(state.shape, F32),
            pltpu.VMEM(state.shape, F32),
            pltpu.VMEM((levels, rows, tile), F32),
            pltpu.VMEM((levels, rows, tile), F32),
            pltpu.VMEM((levels, rows, tile), F32),
            pltpu.VMEM((columns, columns), BF16),
            pltpu.VMEM((columns, columns), BF16),
            pltpu.VMEM((3, tile, columns), BF16),
            pltpu.VMEM((n * wire, tile), F32),
            pltpu.VMEM((n * wire, tile), F32),
            pltpu.VMEM((n, 8, tile), F32),
            pltpu.VMEM((n, 8, tile), F32),
            sems((n,)),
            sems((n,)),
            sems((n,)),
            sems((n,)),
        ]
        + per_batch,
        compiler_params=pltpu.CompilerParams(
            collective_id=0, has_side_effects=True, vmem_limit_bytes=56 * 1024 * 1024
        ),
        cost_estimate=pl.CostEstimate(flops=8 * 10**9, bytes_accessed=6 * 10**6, transcendentals=0),
    )(*operands)


def solution(mesh):
    n_lat, n_lon = mesh.shape["lat"], mesh.shape["lon"]
    in_specs = (P(None, None, "lat", "lon"), P("lat", "lon"), P("lat", "lon"), P(), P("lat", "lon"))
    out_specs = (P(None, None, "lat", "lon"), P(("lat", "lon"), None, None))
    return jax.shard_map(
        functools.partial(per_device, n_lat, n_lon),
        mesh=mesh,
        in_specs=in_specs,
        out_specs=out_specs,
        check_vma=False,
    )
```

```python
import functools
import math

import jax
import jax.numpy as jnp
import ml_dtypes
import numpy as np
from jax import lax
from jax.experimental import pallas as pl
from jax.experimental.pallas import tpu as pltpu
from jax.sharding import PartitionSpec as P

STEPS = 2
KEEP = 64
ADVECT = 0.1
DIFFUSE = 0.1
ROTATE = 0.2
RADIATE = 0.5
FLOOR = 0.25
MESH = pl.DeviceIdType.MESH
F32 = jnp.float32
BF16 = jnp.bfloat16


def filter_tables(fields, tile, n_lon, rank):
    total = tile * n_lon
    ids, waves = np.arange(tile), np.arange(KEEP)
    phase = 2 * np.pi * np.outer(ids, waves) / total
    basis = np.concatenate([np.cos(phase), np.sin(phase[:, 1:])], axis=1)
    basis = basis * np.sqrt(2 / total)
    basis[:, 0] /= np.sqrt(2)
    left = np.linalg.svd(basis, full_matrices=False)[0][:, :rank]
    between = np.zeros((n_lon, rank, n_lon, rank))
    for apart in range(-n_lon + 1, n_lon):
        gap = apart * tile + ids[:, None] - ids[None, :]
        kernel = np.ones(gap.shape) / total
        for wave in range(1, KEEP):
            kernel += (2 / total) * np.cos(2 * np.pi * ((wave * gap) % total) / total)
        block = left.T @ kernel @ left
        for source in range(n_lon):
            if 0 <= source + apart < n_lon:
                between[source, :, source + apart, :] = block.T
    lanes = fields * rank
    analysis = np.zeros((fields, tile, lanes))
    synthesis = np.zeros((lanes, fields, tile))
    for f in range(fields):
        analysis[f, :, f * rank : (f + 1) * rank] = left
        synthesis[f * rank : (f + 1) * rank, f, :] = left.T
    analysis = parts_of(analysis.reshape(fields * tile, lanes))
    between = parts_of(between.reshape(n_lon * rank, n_lon * rank))
    high, low = parts_of(synthesis.reshape(lanes, fields * tile))
    return (
        np.concatenate(analysis, axis=1),
        np.concatenate(between, axis=1),
        np.concatenate([high, high, low], axis=0),
    )


def parts_of(table):
    high = table.astype(ml_dtypes.bfloat16)
    return high, (table - high.astype(np.float64)).astype(ml_dtypes.bfloat16)


def split2(x):
    high = x.astype(BF16)
    return high, (x - high.astype(F32)).astype(BF16)


def dot(a, b):
    return jnp.dot(a, b, preferred_element_type=F32)


def dot_parts(x, table):
    width = table.shape[1] // 2
    high, low = split2(x)
    both = dot(high, table[...])
    return both[:, :width] + both[:, width:] + dot(low, table[:, :width])


def dot_nt(a, b):
    return lax.dot_general(a, b, (((1,), (1,)), ((), ())), preferred_element_type=F32)


def split3(x):
    high = x.astype(BF16)
    rest = x - high.astype(F32)
    middle = rest.astype(BF16)
    low = (rest - middle.astype(F32)).astype(BF16)
    return high, middle, low


def kernel(
    n_lat,
    n_lon,
    batches,
    capacity,
    state_in,
    mixing_in,
    sun_in,
    rows_in,
    map_in,
    analysis_in,
    between_in,
    synthesis_in,
    geometry_in,
    out,
    block_out,
    state,
    mixing,
    sun,
    wanted_rows,
    block_map,
    analysis,
    between,
    synthesis,
    geometry,
    in_sem,
    stepped,
    current,
    ratios,
    inverses,
    heat,
    to_sorted,
    to_slots,
    heat_split,
    heat_send,
    heat_recv,
    slot_send,
    slot_recv,
    slot_ssem,
    slot_rsem,
    heat_ssem,
    heat_rsem,
    *batch_refs,
):
    fields, levels, rows, tile = state.shape
    n = n_lat * n_lon
    columns = rows * tile
    per_peer = columns // n
    rank = tile // fields
    group = tile // fields
    wire = heat_send.shape[0] // n
    lat = lax.axis_index("lat")
    lon = lax.axis_index("lon")
    me = lat * n_lon + lon
    east = lax.rem(lon + 1, n_lon)
    west = lax.rem(lon + n_lon - 1, n_lon)

    sources = (
        state_in,
        mixing_in,
        sun_in,
        rows_in,
        map_in,
        analysis_in,
        between_in,
        synthesis_in,
        geometry_in,
    )
    places = (state, mixing, sun, wanted_rows, block_map, analysis, between, synthesis, geometry)
    loads = [
        pltpu.make_async_copy(src, dst, in_sem.at[k])
        for k, (src, dst) in enumerate(zip(sources, places))
    ]
    for load in loads:
        load.start()

    barrier = pltpu.get_barrier_semaphore()

    @pl.loop(1, n)
    def _(d):
        peer = lax.rem(me + d, n)
        pl.semaphore_signal(
            barrier, inc=1, device_id=(peer // n_lon, lax.rem(peer, n_lon)), device_id_type=MESH
        )

    lane = lax.broadcasted_iota(jnp.int32, (rows, tile), 1)
    row = lax.broadcasted_iota(jnp.int32, (rows, tile), 0)

    class Batch:
        pass

    def make_batch(b):
        first, share = batches[b]
        count = share * n_lon
        (
            lat_send,
            lat_recv,
            lon_send,
            lon_recv,
            z_send,
            z_recv,
            y_send,
            y_recv,
            halo_ssem,
            halo_rsem,
            z_ssem,
            z_rsem,
            y_ssem,
            y_rsem,
            pick,
            spread,
        ) = batch_refs[b * 16 : (b + 1) * 16]
        groups = lon_send.shape[2]
        here = pl.ds(first, count)
        many = z_send.shape[2]
        gathers = capacity < rows

        def one_hot(shape, packed_axis):
            packed = lax.broadcasted_iota(jnp.int32, shape, packed_axis)
            full = lax.broadcasted_iota(jnp.int32, shape, 1 - packed_axis)
            owner = packed // many
            inside = packed - owner * many
            level_in = inside // capacity
            spot = inside - level_in * capacity
            level = full // rows
            row_at = full - level * rows
            place = jnp.full(shape, -1, jnp.int32)
            taken = jnp.int32(0)
            for r in range(rows):
                used = wanted_rows[lat * rows + r]
                place = jnp.where(row_at == r, jnp.where(used == 1, taken, -1), place)
                taken = taken + used
            match = (level == owner * share + level_in) & (place == spot) & (level_in < share)
            return jnp.where(match, 1.0, 0.0).astype(BF16)

        def prepare():
            if gathers:
                pick[...] = one_hot(pick.shape, 0)
                spread[...] = one_hot(spread.shape, 1)

        def halo(t, side):
            if side < 2:
                src, dst = lat_send.at[t, side], lat_recv.at[t, side]
                peer = (lat + (1 if side == 0 else -1), lon)
            else:
                src, dst = lon_send.at[t, side - 2], lon_recv.at[t, side - 2]
                peer = (lat, east if side == 2 else west)
            return pltpu.make_async_remote_copy(
                src_ref=src,
                dst_ref=dst,
                send_sem=halo_ssem.at[t, side],
                recv_sem=halo_rsem.at[t, side],
                device_id=peer,
                device_id_type=MESH,
            )

        def pack(t, src):
            for f in range(fields):
                lat_send[t, 0, f] = src[f, here, rows - 1, :]
                lat_send[t, 1, f] = src[f, here, 0, :]
            for g in range(groups):
                lon_send[t, 0, g] = jnp.zeros((rows, tile), F32)
                lon_send[t, 1, g] = jnp.zeros((rows, tile), F32)
            chunk = math.gcd(math.gcd(count, group), 8)

            @pl.loop(0, count // chunk)
            def _(c):
                g = c * chunk // group
                low = lon_send[t, 1, g]
                high = lon_send[t, 0, g]
                for k in range(chunk):
                    l = c * chunk + k
                    for f in range(fields):
                        x = src[f, first + l]
                        spot = lane == lax.rem(l, group) * fields + f
                        low = jnp.where(spot, jnp.broadcast_to(x[:, :1], x.shape), low)
                        high = jnp.where(spot, jnp.broadcast_to(x[:, tile - 1 :], x.shape), high)
                lon_send[t, 1, g] = low
                lon_send[t, 0, g] = high

        def start_halos(t):
            halo(t, 2).start()
            halo(t, 3).start()

            @pl.when(lat < n_lat - 1)
            def _():
                halo(t, 0).start()

            @pl.when(lat > 0)
            def _():
                halo(t, 1).start()

        def wait_halos(t):
            @pl.when(lat > 0)
            def _():
                halo(t, 0).wait_recv()

            @pl.when(lat == 0)
            def _():
                lat_recv[t, 0] = jnp.zeros(lat_recv.shape[2:], F32)

            @pl.when(lat < n_lat - 1)
            def _():
                halo(t, 1).wait_recv()

            @pl.when(lat == n_lat - 1)
            def _():
                lat_recv[t, 1] = jnp.zeros(lat_recv.shape[2:], F32)

            halo(t, 2).wait_recv()
            halo(t, 3).wait_recv()

        def wait_halo_sends(t):
            @pl.when(lat < n_lat - 1)
            def _():
                halo(t, 0).wait_send()

            @pl.when(lat > 0)
            def _():
                halo(t, 1).wait_send()

            halo(t, 2).wait_send()
            halo(t, 3).wait_send()

        def advance(t, src):
            metric = geometry[lat, 0]
            coriolis = geometry[lat, 1]

            def one(l):
                g = l // group
                from_west = lon_recv[t, 0, g]
                from_east = lon_recv[t, 1, g]
                u = src[0, first + l]
                v = src[1, first + l]
                zonal = u * metric
                made = []
                for f in range(fields):
                    x = src[f, first + l]
                    spot = lax.rem(l, group) * fields + f
                    eastern = jnp.where(
                        lane == tile - 1,
                        pltpu.roll(from_east, tile - 1 - spot, 1),
                        pltpu.roll(x, tile - 1, 1),
                    )
                    western = jnp.where(
                        lane == 0,
                        pltpu.roll(from_west, lax.rem(tile - spot, tile), 1),
                        pltpu.roll(x, 1, 1),
                    )
                    northern = jnp.where(
                        row == rows - 1,
                        lat_recv[t, 1, f, pl.ds(l, 1), :],
                        pltpu.roll(x, rows - 1, 0),
                    )
                    southern = jnp.where(
                        row == 0, lat_recv[t, 0, f, pl.ds(l, 1), :], pltpu.roll(x, 1, 0)
                    )
                    new = x - ADVECT * (zonal * (eastern - western) + v * (northern - southern))
                    new = new + DIFFUSE * (eastern + western + northern + southern - 4.0 * x)
                    if f == 0:
                        new = new + ROTATE * coriolis * v
                    if f == 1:
                        new = new - ROTATE * coriolis * u
                    made.append(new)
                return made

            chunk = math.gcd(count, 4)

            @pl.loop(0, count // chunk)
            def _(c):
                made = [one(c * chunk + k) for k in range(chunk)]
                for k in range(chunk):
                    for f in range(fields):
                        stepped[f, first + c * chunk + k] = made[k][f]

        def z_copy(t, d):
            owner = lax.rem(lon + d, n_lon)
            return pltpu.make_async_remote_copy(
                src_ref=z_send.at[t, owner],
                dst_ref=z_recv.at[t, lon],
                send_sem=z_ssem.at[t, d],
                recv_sem=z_rsem.at[t, d],
                device_id=(lat, owner),
                device_id_type=MESH,
            )

        def y_copy(t, d):
            source = lax.rem(lon + d, n_lon)
            return pltpu.make_async_remote_copy(
                src_ref=y_send.at[t, source],
                dst_ref=y_recv.at[t, lon],
                send_sem=y_ssem.at[t, d],
                recv_sem=y_rsem.at[t, d],
                device_id=(lat, source),
                device_id_type=MESH,
            )

        def analyse(t):
            parts = [stepped[f, here].reshape(count * rows, tile) for f in range(fields)]
            z = dot_parts(jnp.concatenate(parts, axis=1), analysis)
            if gathers:
                high, low = split2(z)
                z = dot(pick[...], high) + dot(pick[...], low)
            z_send[t] = z.reshape(n_lon, many, tile)

            @pl.loop(1, n_lon)
            def _(d):
                z_copy(t, d).start()

            z_recv[t, lon] = z_send[t, lon]

        def own(t):
            @pl.loop(1, n_lon)
            def _(d):
                z_copy(t, d).wait_recv()

            wide = lax.broadcasted_iota(jnp.int32, (many, tile), 1) // rank
            halves = []
            for h in range(n_lon // fields):
                got = [z_recv[t, h * fields + k] for k in range(fields)]
                per_field = []
                for f in range(fields):
                    total = None
                    for k in range(fields):
                        shift = (rank * (k - f)) % tile
                        moved = pltpu.roll(got[k], shift, 1) if shift else got[k]
                        total = moved if k == 0 else jnp.where(wide == k, moved, total)
                    per_field.append(total)
                halves.append(jnp.concatenate(per_field, axis=0))
            y = dot_parts(jnp.concatenate(halves, axis=1), between)
            for p in range(n_lon):
                h, k = p // fields, p % fields
                total = None
                for f in range(fields):
                    piece = y[f * many : (f + 1) * many, h * tile : (h + 1) * tile]
                    shift = (rank * (f - k)) % tile
                    piece = pltpu.roll(piece, shift, 1) if shift else piece
                    total = piece if f == 0 else jnp.where(wide == f, piece, total)
                y_send[t, p] = total

            @pl.loop(1, n_lon)
            def _(d):
                y_copy(t, d).start()

            y_recv[t, lon] = y_send[t, lon]

        def synthesise(t):
            wanted = jnp.zeros((rows, tile), jnp.int32)
            for r in range(rows):
                wanted = jnp.where(row == r, wanted_rows[lat * rows + r], wanted)
            filtered = (wanted == 1)[None]

            @pl.loop(1, n_lon)
            def _(d):
                y_copy(t, d).wait_recv()

            high, low = split2(y_recv[t].reshape(n_lon * many, tile))
            if gathers:
                high = dot(spread[...], high).astype(BF16)
                low = dot(spread[...], low).astype(BF16)
            smooth = dot(jnp.concatenate([high, low, high], axis=1), synthesis[...])
            for f in range(fields):
                piece = smooth[:, f * tile : (f + 1) * tile].reshape(count, rows, tile)
                current[f, here] = jnp.where(filtered, piece, stepped[f, here])

        def wait_sends(t):
            wait_halo_sends(t)

            @pl.loop(1, n_lon)
            def _(d):
                z_copy(t, d).wait_send()
                y_copy(t, d).wait_send()

        batch = Batch()
        batch.first, batch.count = first, count
        batch.pack, batch.start_halos, batch.wait_halos = pack, start_halos, wait_halos
        batch.advance, batch.analyse, batch.own = advance, analyse, own
        batch.synthesise, batch.wait_sends = synthesise, wait_sends
        batch.prepare = prepare
        return batch

    def slot_copy(d):
        peer = lax.rem(me + d, n)
        return pltpu.make_async_remote_copy(
            src_ref=slot_send.at[peer],
            dst_ref=slot_recv.at[me],
            send_sem=slot_ssem.at[d],
            recv_sem=slot_rsem.at[d],
            device_id=(peer // n_lon, lax.rem(peer, n_lon)),
            device_id_type=MESH,
        )

    def heat_copy(d):
        peer = lax.rem(me + d, n)
        there = pl.ds(pl.multiple_of(peer * wire, wire), wire)
        here = pl.ds(pl.multiple_of(me * wire, wire), wire)
        return pltpu.make_async_remote_copy(
            src_ref=heat_send.at[there],
            dst_ref=heat_recv.at[here],
            send_sem=heat_ssem.at[d],
            recv_sem=heat_rsem.at[d],
            device_id=(peer // n_lon, lax.rem(peer, n_lon)),
            device_id_type=MESH,
        )

    def sort_columns():
        mapped = block_map[...].astype(F32)
        target = jnp.floor((mapped + 0.5) * (1.0 / columns))
        slot = mapped - target * columns
        slot_high = slot.astype(BF16)
        slot_low = (slot - slot_high.astype(F32)).astype(BF16)
        peers = lax.broadcasted_iota(jnp.int32, (n, tile), 0).astype(F32)
        before = lax.broadcasted_iota(jnp.int32, (tile, tile), 0)
        after = lax.broadcasted_iota(jnp.int32, (tile, tile), 1)
        earlier = (before < after).astype(F32).astype(BF16)
        positions = lax.broadcasted_iota(jnp.int32, (columns, tile), 0).astype(F32)
        places = lax.broadcasted_iota(jnp.int32, (tile, tile), 0).astype(F32)
        base = jnp.zeros((n, 1), F32)
        slots = jnp.zeros((n, tile), F32)
        for r in range(rows):
            hit = (peers == target[r : r + 1]).astype(F32)
            prefix = dot(hit.astype(BF16), earlier) + base
            base = base + jnp.sum(hit, axis=1, keepdims=True)
            order = jnp.sum(hit * prefix, axis=0, keepdims=True)
            spot = target[r : r + 1] * per_peer + order
            to_sorted[:, r * tile : (r + 1) * tile] = (positions == spot).astype(F32).astype(BF16)
            named = (places == order).astype(F32)
            for part in (slot_high, slot_low):
                weighted = (named * part[r : r + 1].astype(F32)).astype(BF16)
                slots = slots + dot_nt(hit.astype(BF16), weighted)
        slot_send[...] = jnp.broadcast_to(slots[:, None, :], slot_send.shape)
        slot_recv[me] = slot_send[me]

        @pl.loop(1, n)
        def _(d):
            slot_copy(d).start()

    def place_columns():
        @pl.loop(1, n)
        def _(d):
            slot_copy(d).wait_recv()

        names = slot_recv[:, 0, :].T[:per_peer]
        join = max(1, 16 // per_peer)
        size = join * per_peer
        ids = lax.broadcasted_iota(jnp.int32, (size, columns), 1).astype(F32)
        for k in range(n // join):
            picked = [names[:, s : s + 1] for s in range(k * join, (k + 1) * join)]
            column = picked[0] if join == 1 else jnp.concatenate(picked, axis=0)
            to_slots[k * size : (k + 1) * size, :] = (ids == column).astype(F32).astype(BF16)

    def ratios_of_levels():
        mix = mixing[...]

        def body(l, upper):
            at_end = jnp.logical_or(l == 0, l == levels - 1)
            diagonal = 1.0 + jnp.where(at_end, 1.0, 2.0) * mix
            inverse = 1.0 / (diagonal + mix * upper)
            ratio = -mix * inverse
            inverses[l] = inverse
            ratios[l] = ratio
            return ratio

        lax.fori_loop(0, levels, body, jnp.zeros((rows, tile), F32))

    zeros = tuple(jnp.zeros((rows, tile), F32) for f in range(fields))

    def mix_down(batch, carried):
        mix = mixing[...]

        def forward(l, above):
            inverse = inverses[l]
            values = tuple((current[f, l] + mix * above[f]) * inverse for f in range(fields))
            for f in range(fields):
                out[f, l] = values[f]
            return values

        return lax.fori_loop(batch.first, batch.first + batch.count, forward, carried, unroll=8)

    def mix_up():
        warming = RADIATE * sun[...]

        def backward(step, below):
            l = levels - 1 - step
            ratio = ratios[l]
            solved = tuple(out[f, l] - ratio * below[f] for f in range(fields))
            for f in range(fields):
                if f == 2:
                    warmed = solved[2] + warming * solved[3]
                    out[2, l] = warmed
                    heat[l] = warmed - current[2, l]
                else:
                    out[f, l] = solved[f]
            return solved

        lax.fori_loop(0, levels, backward, zeros, unroll=8)

    spill = per_peer - wire
    half = levels // 2

    def send_heat():
        for r in range(rows):
            for k, part in enumerate(split3(heat[:, r, :])):
                heat_split[k, :levels, r * tile : (r + 1) * tile] = part
                if levels < tile:
                    heat_split[k, levels:, r * tile : (r + 1) * tile] = jnp.zeros(
                        (tile - levels, tile), BF16
                    )
        table = heat_split[...].reshape(3 * tile, columns)
        sorted3 = dot_nt(to_sorted[...], table)
        sent = sorted3[:, :tile] + sorted3[:, tile : 2 * tile] + sorted3[:, 2 * tile :]
        if spill:
            spots = lax.broadcasted_iota(jnp.int32, (spill, tile), 1)
            free = spots >= levels
            pieces = []
            for p in range(n):
                base = p * per_peer
                extra = sent[base + wire : base + per_peer]
                pieces.append(
                    jnp.where(free, pltpu.roll(extra, levels, 1), sent[base : base + spill])
                )
                pieces.append(
                    jnp.where(
                        free,
                        pltpu.roll(extra, levels - half, 1),
                        sent[base + spill : base + 2 * spill],
                    )
                )
                pieces.append(sent[base + 2 * spill : base + wire])
            sent = jnp.concatenate(pieces, axis=0)
        heat_send[...] = sent

        @pl.loop(1, n)
        def _(d):
            heat_copy(d).start()

        mine = pl.ds(pl.multiple_of(me * wire, wire), wire)
        heat_recv[mine] = heat_send[mine]

    def place_heat():
        @pl.loop(1, n)
        def _(d):
            heat_copy(d).wait_recv()

        got = heat_recv[...]
        if spill:
            spots = lax.broadcasted_iota(jnp.int32, (spill, tile), 1)
            pieces = []
            for p in range(n):
                message = got[p * wire : (p + 1) * wire]
                extra = jnp.where(
                    spots < half,
                    pltpu.roll(message[:spill], tile - levels, 1),
                    pltpu.roll(message[spill : 2 * spill], tile - levels + half, 1),
                )
                pieces += [message, extra]
            got = jnp.concatenate(pieces, axis=0)
        table = jnp.concatenate(split3(got.T), axis=0)
        placed = dot(table, to_slots[...])
        total = placed[:tile] + placed[tile : 2 * tile] + placed[2 * tile :]
        block_out[0] = total[:levels]

    work = [make_batch(b) for b in range(len(batches))]
    loads[0].wait()
    for batch in work:
        batch.pack(0, state)
    pl.semaphore_wait(barrier, n - 1)
    for batch in work:
        batch.start_halos(0)
    for load in loads[1:]:
        load.wait()
    for batch in work:
        batch.prepare()
    sort_columns()
    for t in range(STEPS):
        source = state if t == 0 else current
        for batch in work:
            batch.wait_halos(t)
            batch.advance(t, source)
            batch.analyse(t)
        if t == 0:
            ratios_of_levels()
        for batch in work:
            batch.own(t)
        if t == 0:
            place_columns()
        carried = zeros
        for batch in work:
            batch.synthesise(t)
            if t + 1 < STEPS:
                batch.pack(t + 1, current)
                batch.start_halos(t + 1)
            else:
                carried = mix_down(batch, carried)
    mix_up()
    send_heat()
    for batch in work:
        for t in range(STEPS):
            batch.wait_sends(t)
    place_heat()

    @pl.loop(1, n)
    def _(d):
        slot_copy(d).wait_send()
        heat_copy(d).wait_send()


def split_levels(share, capacity):
    large = share - share // 2
    if large * capacity % 8 and large + 1 < share and (large + 1) * capacity % 8 == 0:
        large += 1
    return large, share - large


def program(n_lat, n_lon, capacity, state, mixing, insolation, filter_rows, block_map):
    fields, levels, rows, tile = state.shape
    n = n_lat * n_lon
    columns = rows * tile
    per_peer = columns // n
    rank = tile // fields
    large, small = split_levels(levels // n_lon, capacity)
    batches = ((0, large), (large * n_lon, small))
    analysis, between, synthesis = filter_tables(fields, tile, n_lon, rank)
    total_rows = rows * n_lat
    latitude = (np.arange(total_rows) + 0.5) * (math.pi / total_rows) - 0.5 * math.pi
    by_row = np.stack([1.0 / np.maximum(np.cos(latitude), FLOOR), np.sin(latitude)])
    by_row = by_row.reshape(2, n_lat, rows, 1).transpose(1, 0, 2, 3)
    geometry = np.broadcast_to(by_row, (n_lat, 2, rows, tile)).astype(np.float32)
    spare = per_peer % 32 == 0 and levels % 2 == 0 and levels + levels // 2 <= tile
    wire = per_peer * 3 // 4 if spare else per_peer
    vmem = pl.BlockSpec(memory_space=pltpu.VMEM)
    anywhere = pl.BlockSpec(memory_space=pl.ANY)
    sems = pltpu.SemaphoreType.DMA
    operands = (
        state,
        mixing,
        insolation,
        filter_rows,
        block_map,
        analysis,
        between,
        synthesis,
        geometry,
    )
    places = [
        pltpu.SMEM(a.shape, a.dtype) if a is filter_rows else pltpu.VMEM(a.shape, a.dtype)
        for a in operands
    ]
    per_batch = []
    for _, part in batches:
        count = part * n_lon
        edge = (STEPS, 2, fields, count, tile)
        side = (STEPS, 2, -(-count * fields // tile), rows, tile)
        many = -(-part * capacity // 8) * 8
        block = (STEPS, n_lon, many, tile)
        for shape in (edge, edge, side, side, block, block, block, block):
            per_batch.append(pltpu.VMEM(shape, F32))
        per_batch += [sems((STEPS, 4))] * 2 + [sems((STEPS, n_lon))] * 4
        per_batch.append(pltpu.VMEM((n_lon * many, count * rows), BF16))
        per_batch.append(pltpu.VMEM((count * rows, n_lon * many), BF16))
    return pl.pallas_call(
        functools.partial(kernel, n_lat, n_lon, batches, capacity),
        out_shape=(
            jax.ShapeDtypeStruct(state.shape, F32),
            jax.ShapeDtypeStruct((1, levels, columns), F32),
        ),
        in_specs=[anywhere] * len(operands),
        out_specs=(vmem, vmem),
        scratch_shapes=places
        + [
            sems((len(operands),)),
            pltpu.VMEM(state.shape, F32),
            pltpu.VMEM(state.shape, F32),
            pltpu.VMEM((levels, rows, tile), F32),
            pltpu.VMEM((levels, rows, tile), F32),
            pltpu.VMEM((levels, rows, tile), F32),
            pltpu.VMEM((columns, columns), BF16),
            pltpu.VMEM((columns, columns), BF16),
            pltpu.VMEM((3, tile, columns), BF16),
            pltpu.VMEM((n * wire, tile), F32),
            pltpu.VMEM((n * wire, tile), F32),
            pltpu.VMEM((n, 8, tile), F32),
            pltpu.VMEM((n, 8, tile), F32),
            sems((n,)),
            sems((n,)),
            sems((n,)),
            sems((n,)),
        ]
        + per_batch,
        compiler_params=pltpu.CompilerParams(
            collective_id=capacity, has_side_effects=True, vmem_limit_bytes=56 * 1024 * 1024
        ),
        cost_estimate=pl.CostEstimate(flops=8 * 10**9, bytes_accessed=6 * 10**6, transcendentals=0),
    )(*operands)


def per_device(n_lat, n_lon, state, mixing, insolation, filter_rows, block_map):
    rows = state.shape[2]
    most = jnp.max(jnp.sum(filter_rows.reshape(n_lat, rows), axis=1))
    return lax.cond(
        most <= rows // 2,
        functools.partial(program, n_lat, n_lon, rows // 2),
        functools.partial(program, n_lat, n_lon, rows),
        state,
        mixing,
        insolation,
        filter_rows,
        block_map,
    )


def solution(mesh):
    n_lat, n_lon = mesh.shape["lat"], mesh.shape["lon"]
    in_specs = (P(None, None, "lat", "lon"), P("lat", "lon"), P("lat", "lon"), P(), P("lat", "lon"))
    out_specs = (P(None, None, "lat", "lon"), P(("lat", "lon"), None, None))
    return jax.shard_map(
        functools.partial(per_device, n_lat, n_lon),
        mesh=mesh,
        in_specs=in_specs,
        out_specs=out_specs,
        check_vma=False,
    )
```

```python
import functools
import math

import jax
import jax.numpy as jnp
import ml_dtypes
import numpy as np
from jax import lax
from jax.experimental import pallas as pl
from jax.experimental.pallas import tpu as pltpu
from jax.sharding import PartitionSpec as P

STEPS = 2
KEEP = 64
ADVECT = 0.1
DIFFUSE = 0.1
ROTATE = 0.2
RADIATE = 0.5
FLOOR = 0.25
MESH = pl.DeviceIdType.MESH
F32 = jnp.float32
BF16 = jnp.bfloat16


def filter_tables(fields, tile, n_lon, rank):
    total = tile * n_lon
    ids, waves = np.arange(tile), np.arange(KEEP)
    phase = 2 * np.pi * np.outer(ids, waves) / total
    basis = np.concatenate([np.cos(phase), np.sin(phase[:, 1:])], axis=1)
    basis = basis * np.sqrt(2 / total)
    basis[:, 0] /= np.sqrt(2)
    left = np.linalg.svd(basis, full_matrices=False)[0][:, :rank]
    between = np.zeros((n_lon, rank, n_lon, rank))
    for apart in range(-n_lon + 1, n_lon):
        gap = apart * tile + ids[:, None] - ids[None, :]
        kernel = np.ones(gap.shape) / total
        for wave in range(1, KEEP):
            kernel += (2 / total) * np.cos(2 * np.pi * ((wave * gap) % total) / total)
        block = left.T @ kernel @ left
        for source in range(n_lon):
            if 0 <= source + apart < n_lon:
                between[source, :, source + apart, :] = block.T
    lanes = fields * rank
    analysis = np.zeros((fields, tile, lanes))
    synthesis = np.zeros((lanes, fields, tile))
    for f in range(fields):
        analysis[f, :, f * rank : (f + 1) * rank] = left
        synthesis[f * rank : (f + 1) * rank, f, :] = left.T
    analysis = parts_of(analysis.reshape(fields * tile, lanes))
    between = parts_of(between.reshape(n_lon * rank, n_lon * rank))
    high, low = parts_of(synthesis.reshape(lanes, fields * tile))
    return (
        np.concatenate(analysis, axis=1),
        np.concatenate(between, axis=1),
        np.concatenate([high, high, low], axis=0),
    )


def parts_of(table):
    high = table.astype(ml_dtypes.bfloat16)
    return high, (table - high.astype(np.float64)).astype(ml_dtypes.bfloat16)


def split2(x):
    high = x.astype(BF16)
    return high, (x - high.astype(F32)).astype(BF16)


def dot(a, b):
    return jnp.dot(a, b, preferred_element_type=F32)


def dot_parts(x, table):
    width = table.shape[1] // 2
    high, low = split2(x)
    both = dot(high, table[...])
    return both[:, :width] + both[:, width:] + dot(low, table[:, :width])


def dot_nt(a, b):
    return lax.dot_general(a, b, (((1,), (1,)), ((), ())), preferred_element_type=F32)


def split3(x):
    high = x.astype(BF16)
    rest = x - high.astype(F32)
    middle = rest.astype(BF16)
    low = (rest - middle.astype(F32)).astype(BF16)
    return high, middle, low


def kernel(
    n_lat,
    n_lon,
    batches,
    capacity,
    state_in,
    mixing_in,
    sun_in,
    rows_in,
    map_in,
    analysis_in,
    between_in,
    synthesis_in,
    geometry_in,
    out,
    block_out,
    state,
    mixing,
    sun,
    wanted_rows,
    block_map,
    analysis,
    between,
    synthesis,
    geometry,
    in_sem,
    stepped,
    current,
    ratios,
    inverses,
    heat,
    to_sorted,
    to_slots,
    heat_split,
    heat_send,
    heat_recv,
    slot_send,
    slot_recv,
    slot_ssem,
    slot_rsem,
    heat_ssem,
    heat_rsem,
    *batch_refs,
):
    fields, levels, rows, tile = state.shape
    n = n_lat * n_lon
    columns = rows * tile
    per_peer = columns // n
    rank = tile // fields
    group = tile // fields
    wire = heat_send.shape[0] // n
    lat = lax.axis_index("lat")
    lon = lax.axis_index("lon")
    me = lat * n_lon + lon
    east = lax.rem(lon + 1, n_lon)
    west = lax.rem(lon + n_lon - 1, n_lon)

    sources = (
        state_in,
        mixing_in,
        sun_in,
        rows_in,
        map_in,
        analysis_in,
        between_in,
        synthesis_in,
        geometry_in,
    )
    places = (state, mixing, sun, wanted_rows, block_map, analysis, between, synthesis, geometry)
    loads = [
        pltpu.make_async_copy(src, dst, in_sem.at[k])
        for k, (src, dst) in enumerate(zip(sources, places))
    ]
    for load in loads:
        load.start()

    barrier = pltpu.get_barrier_semaphore()

    @pl.loop(1, n)
    def _(d):
        peer = lax.rem(me + d, n)
        pl.semaphore_signal(
            barrier, inc=1, device_id=(peer // n_lon, lax.rem(peer, n_lon)), device_id_type=MESH
        )

    lane = lax.broadcasted_iota(jnp.int32, (rows, tile), 1)
    row = lax.broadcasted_iota(jnp.int32, (rows, tile), 0)

    class Batch:
        pass

    def make_batch(b):
        first, share = batches[b]
        count = share * n_lon
        (
            lat_send,
            lat_recv,
            lon_send,
            lon_recv,
            z_send,
            z_recv,
            y_send,
            y_recv,
            halo_ssem,
            halo_rsem,
            z_ssem,
            z_rsem,
            y_ssem,
            y_rsem,
            pick,
            spread,
        ) = batch_refs[b * 16 : (b + 1) * 16]
        groups = lon_send.shape[2]
        here = pl.ds(first, count)
        many = z_send.shape[2]
        gathers = capacity < rows

        def one_hot(shape, packed_axis):
            packed = lax.broadcasted_iota(jnp.int32, shape, packed_axis)
            full = lax.broadcasted_iota(jnp.int32, shape, 1 - packed_axis)
            owner = packed // many
            inside = packed - owner * many
            level_in = inside // capacity
            spot = inside - level_in * capacity
            level = full // rows
            row_at = full - level * rows
            place = jnp.full(shape, -1, jnp.int32)
            taken = jnp.int32(0)
            for r in range(rows):
                used = wanted_rows[lat * rows + r]
                place = jnp.where(row_at == r, jnp.where(used == 1, taken, -1), place)
                taken = taken + used
            match = (level == owner * share + level_in) & (place == spot) & (level_in < share)
            return jnp.where(match, 1.0, 0.0).astype(BF16)

        def prepare():
            if gathers:
                pick[...] = one_hot(pick.shape, 0)
                spread[...] = one_hot(spread.shape, 1)

        def halo(t, side):
            if side < 2:
                src, dst = lat_send.at[t, side], lat_recv.at[t, side]
                peer = (lat + (1 if side == 0 else -1), lon)
            else:
                src, dst = lon_send.at[t, side - 2], lon_recv.at[t, side - 2]
                peer = (lat, east if side == 2 else west)
            return pltpu.make_async_remote_copy(
                src_ref=src,
                dst_ref=dst,
                send_sem=halo_ssem.at[t, side],
                recv_sem=halo_rsem.at[t, side],
                device_id=peer,
                device_id_type=MESH,
            )

        def pack(t, src):
            for f in range(fields):
                lat_send[t, 0, f] = src[f, here, rows - 1, :]
                lat_send[t, 1, f] = src[f, here, 0, :]
            for g in range(groups):
                lon_send[t, 0, g] = jnp.zeros((rows, tile), F32)
                lon_send[t, 1, g] = jnp.zeros((rows, tile), F32)
            chunk = math.gcd(math.gcd(count, group), 8)

            @pl.loop(0, count // chunk)
            def _(c):
                g = c * chunk // group
                low = lon_send[t, 1, g]
                high = lon_send[t, 0, g]
                for k in range(chunk):
                    l = c * chunk + k
                    for f in range(fields):
                        x = src[f, first + l]
                        spot = lane == lax.rem(l, group) * fields + f
                        low = jnp.where(spot, jnp.broadcast_to(x[:, :1], x.shape), low)
                        high = jnp.where(spot, jnp.broadcast_to(x[:, tile - 1 :], x.shape), high)
                lon_send[t, 1, g] = low
                lon_send[t, 0, g] = high

        def start_halos(t):
            halo(t, 2).start()
            halo(t, 3).start()

            @pl.when(lat < n_lat - 1)
            def _():
                halo(t, 0).start()

            @pl.when(lat > 0)
            def _():
                halo(t, 1).start()

        def wait_halos(t):
            @pl.when(lat > 0)
            def _():
                halo(t, 0).wait_recv()

            @pl.when(lat == 0)
            def _():
                lat_recv[t, 0] = jnp.zeros(lat_recv.shape[2:], F32)

            @pl.when(lat < n_lat - 1)
            def _():
                halo(t, 1).wait_recv()

            @pl.when(lat == n_lat - 1)
            def _():
                lat_recv[t, 1] = jnp.zeros(lat_recv.shape[2:], F32)

            halo(t, 2).wait_recv()
            halo(t, 3).wait_recv()

        def wait_halo_sends(t):
            @pl.when(lat < n_lat - 1)
            def _():
                halo(t, 0).wait_send()

            @pl.when(lat > 0)
            def _():
                halo(t, 1).wait_send()

            halo(t, 2).wait_send()
            halo(t, 3).wait_send()

        def advance(t, src):
            metric = geometry[lat, 0]
            coriolis = geometry[lat, 1]

            def one(l):
                g = l // group
                from_west = lon_recv[t, 0, g]
                from_east = lon_recv[t, 1, g]
                u = src[0, first + l]
                v = src[1, first + l]
                zonal = u * metric
                made = []
                for f in range(fields):
                    x = src[f, first + l]
                    spot = lax.rem(l, group) * fields + f
                    eastern = jnp.where(
                        lane == tile - 1,
                        pltpu.roll(from_east, tile - 1 - spot, 1),
                        pltpu.roll(x, tile - 1, 1),
                    )
                    western = jnp.where(
                        lane == 0,
                        pltpu.roll(from_west, lax.rem(tile - spot, tile), 1),
                        pltpu.roll(x, 1, 1),
                    )
                    northern = jnp.where(
                        row == rows - 1,
                        lat_recv[t, 1, f, pl.ds(l, 1), :],
                        pltpu.roll(x, rows - 1, 0),
                    )
                    southern = jnp.where(
                        row == 0, lat_recv[t, 0, f, pl.ds(l, 1), :], pltpu.roll(x, 1, 0)
                    )
                    new = x - ADVECT * (zonal * (eastern - western) + v * (northern - southern))
                    new = new + DIFFUSE * (eastern + western + northern + southern - 4.0 * x)
                    if f == 0:
                        new = new + ROTATE * coriolis * v
                    if f == 1:
                        new = new - ROTATE * coriolis * u
                    made.append(new)
                return made

            chunk = math.gcd(count, 4)

            @pl.loop(0, count // chunk)
            def _(c):
                made = [one(c * chunk + k) for k in range(chunk)]
                for k in range(chunk):
                    for f in range(fields):
                        stepped[f, first + c * chunk + k] = made[k][f]

        def z_copy(t, d):
            owner = lax.rem(lon + d, n_lon)
            return pltpu.make_async_remote_copy(
                src_ref=z_send.at[t, owner],
                dst_ref=z_recv.at[t, lon],
                send_sem=z_ssem.at[t, d],
                recv_sem=z_rsem.at[t, d],
                device_id=(lat, owner),
                device_id_type=MESH,
            )

        def y_copy(t, d):
            source = lax.rem(lon + d, n_lon)
            return pltpu.make_async_remote_copy(
                src_ref=y_send.at[t, source],
                dst_ref=y_recv.at[t, lon],
                send_sem=y_ssem.at[t, d],
                recv_sem=y_rsem.at[t, d],
                device_id=(lat, source),
                device_id_type=MESH,
            )

        def analyse(t):
            parts = [stepped[f, here].reshape(count * rows, tile) for f in range(fields)]
            z = dot_parts(jnp.concatenate(parts, axis=1), analysis)
            if gathers:
                high, low = split2(z)
                z = dot(pick[...], high) + dot(pick[...], low)
            z_send[t] = z.reshape(n_lon, many, tile)

            @pl.loop(1, n_lon)
            def _(d):
                z_copy(t, d).start()

            z_recv[t, lon] = z_send[t, lon]

        def own(t):
            @pl.loop(1, n_lon)
            def _(d):
                z_copy(t, d).wait_recv()

            wide = lax.broadcasted_iota(jnp.int32, (many, tile), 1) // rank
            halves = []
            for h in range(n_lon // fields):
                got = [z_recv[t, h * fields + k] for k in range(fields)]
                per_field = []
                for f in range(fields):
                    total = None
                    for k in range(fields):
                        shift = (rank * (k - f)) % tile
                        moved = pltpu.roll(got[k], shift, 1) if shift else got[k]
                        total = moved if k == 0 else jnp.where(wide == k, moved, total)
                    per_field.append(total)
                halves.append(jnp.concatenate(per_field, axis=0))
            y = dot_parts(jnp.concatenate(halves, axis=1), between)
            for p in range(n_lon):
                h, k = p // fields, p % fields
                total = None
                for f in range(fields):
                    piece = y[f * many : (f + 1) * many, h * tile : (h + 1) * tile]
                    shift = (rank * (f - k)) % tile
                    piece = pltpu.roll(piece, shift, 1) if shift else piece
                    total = piece if f == 0 else jnp.where(wide == f, piece, total)
                y_send[t, p] = total

            @pl.loop(1, n_lon)
            def _(d):
                y_copy(t, d).start()

            y_recv[t, lon] = y_send[t, lon]

        def synthesise(t):
            wanted = jnp.zeros((rows, tile), jnp.int32)
            for r in range(rows):
                wanted = jnp.where(row == r, wanted_rows[lat * rows + r], wanted)
            filtered = (wanted == 1)[None]

            @pl.loop(1, n_lon)
            def _(d):
                y_copy(t, d).wait_recv()

            high, low = split2(y_recv[t].reshape(n_lon * many, tile))
            if gathers:
                high = dot(spread[...], high).astype(BF16)
                low = dot(spread[...], low).astype(BF16)
            smooth = dot(jnp.concatenate([high, low, high], axis=1), synthesis[...])
            for f in range(fields):
                piece = smooth[:, f * tile : (f + 1) * tile].reshape(count, rows, tile)
                current[f, here] = jnp.where(filtered, piece, stepped[f, here])

        def wait_sends(t):
            wait_halo_sends(t)

            @pl.loop(1, n_lon)
            def _(d):
                z_copy(t, d).wait_send()
                y_copy(t, d).wait_send()

        batch = Batch()
        batch.first, batch.count = first, count
        batch.pack, batch.start_halos, batch.wait_halos = pack, start_halos, wait_halos
        batch.advance, batch.analyse, batch.own = advance, analyse, own
        batch.synthesise, batch.wait_sends = synthesise, wait_sends
        batch.prepare = prepare
        return batch

    def slot_copy(d):
        peer = lax.rem(me + d, n)
        return pltpu.make_async_remote_copy(
            src_ref=slot_send.at[peer],
            dst_ref=slot_recv.at[me],
            send_sem=slot_ssem.at[d],
            recv_sem=slot_rsem.at[d],
            device_id=(peer // n_lon, lax.rem(peer, n_lon)),
            device_id_type=MESH,
        )

    def heat_copy(d):
        peer = lax.rem(me + d, n)
        there = pl.ds(pl.multiple_of(peer * wire, wire), wire)
        here = pl.ds(pl.multiple_of(me * wire, wire), wire)
        return pltpu.make_async_remote_copy(
            src_ref=heat_send.at[there],
            dst_ref=heat_recv.at[here],
            send_sem=heat_ssem.at[d],
            recv_sem=heat_rsem.at[d],
            device_id=(peer // n_lon, lax.rem(peer, n_lon)),
            device_id_type=MESH,
        )

    def sort_columns():
        mapped = block_map[...].astype(F32)
        target = jnp.floor((mapped + 0.5) * (1.0 / columns))
        slot = mapped - target * columns
        slot_high = slot.astype(BF16)
        slot_low = (slot - slot_high.astype(F32)).astype(BF16)
        peers = lax.broadcasted_iota(jnp.int32, (n, tile), 0).astype(F32)
        before = lax.broadcasted_iota(jnp.int32, (tile, tile), 0)
        after = lax.broadcasted_iota(jnp.int32, (tile, tile), 1)
        earlier = (before < after).astype(F32).astype(BF16)
        positions = lax.broadcasted_iota(jnp.int32, (columns, tile), 0).astype(F32)
        places = lax.broadcasted_iota(jnp.int32, (tile, tile), 0).astype(F32)
        base = jnp.zeros((n, 1), F32)
        slots = jnp.zeros((n, tile), F32)
        for r in range(rows):
            hit = (peers == target[r : r + 1]).astype(F32)
            prefix = dot(hit.astype(BF16), earlier) + base
            base = base + jnp.sum(hit, axis=1, keepdims=True)
            order = jnp.sum(hit * prefix, axis=0, keepdims=True)
            spot = target[r : r + 1] * per_peer + order
            to_sorted[:, r * tile : (r + 1) * tile] = (positions == spot).astype(F32).astype(BF16)
            named = (places == order).astype(F32)
            for part in (slot_high, slot_low):
                weighted = (named * part[r : r + 1].astype(F32)).astype(BF16)
                slots = slots + dot_nt(hit.astype(BF16), weighted)
        slot_send[...] = jnp.broadcast_to(slots[:, None, :], slot_send.shape)
        slot_recv[me] = slot_send[me]

        @pl.loop(1, n)
        def _(d):
            slot_copy(d).start()

    def place_columns():
        @pl.loop(1, n)
        def _(d):
            slot_copy(d).wait_recv()

        names = slot_recv[:, 0, :].T[:per_peer]
        join = max(1, 16 // per_peer)
        size = join * per_peer
        ids = lax.broadcasted_iota(jnp.int32, (size, columns), 1).astype(F32)
        for k in range(n // join):
            picked = [names[:, s : s + 1] for s in range(k * join, (k + 1) * join)]
            column = picked[0] if join == 1 else jnp.concatenate(picked, axis=0)
            to_slots[k * size : (k + 1) * size, :] = (ids == column).astype(F32).astype(BF16)

    def ratios_of_levels():
        mix = mixing[...]

        def body(l, upper):
            at_end = jnp.logical_or(l == 0, l == levels - 1)
            diagonal = 1.0 + jnp.where(at_end, 1.0, 2.0) * mix
            inverse = 1.0 / (diagonal + mix * upper)
            ratio = -mix * inverse
            inverses[l] = inverse
            ratios[l] = ratio
            return ratio

        lax.fori_loop(0, levels, body, jnp.zeros((rows, tile), F32))

    zeros = tuple(jnp.zeros((rows, tile), F32) for f in range(fields))

    def mix_down(batch, carried):
        mix = mixing[...]

        def forward(l, above):
            inverse = inverses[l]
            values = tuple((current[f, l] + mix * above[f]) * inverse for f in range(fields))
            for f in range(fields):
                out[f, l] = values[f]
            return values

        return lax.fori_loop(batch.first, batch.first + batch.count, forward, carried, unroll=8)

    def mix_up():
        warming = RADIATE * sun[...]

        def backward(step, below):
            l = levels - 1 - step
            ratio = ratios[l]
            solved = tuple(out[f, l] - ratio * below[f] for f in range(fields))
            for f in range(fields):
                if f == 2:
                    warmed = solved[2] + warming * solved[3]
                    out[2, l] = warmed
                    heat[l] = warmed - current[2, l]
                else:
                    out[f, l] = solved[f]
            return solved

        lax.fori_loop(0, levels, backward, zeros, unroll=8)

    spill = per_peer - wire
    half = levels // 2

    def send_heat():
        for r in range(rows):
            for k, part in enumerate(split3(heat[:, r, :])):
                heat_split[k, :levels, r * tile : (r + 1) * tile] = part
                if levels < tile:
                    heat_split[k, levels:, r * tile : (r + 1) * tile] = jnp.zeros(
                        (tile - levels, tile), BF16
                    )
        table = heat_split[...].reshape(3 * tile, columns)
        sorted3 = dot_nt(to_sorted[...], table)
        sent = sorted3[:, :tile] + sorted3[:, tile : 2 * tile] + sorted3[:, 2 * tile :]
        if spill:
            spots = lax.broadcasted_iota(jnp.int32, (spill, tile), 1)
            free = spots >= levels
            pieces = []
            for p in range(n):
                base = p * per_peer
                extra = sent[base + wire : base + per_peer]
                pieces.append(
                    jnp.where(free, pltpu.roll(extra, levels, 1), sent[base : base + spill])
                )
                pieces.append(
                    jnp.where(
                        free,
                        pltpu.roll(extra, levels - half, 1),
                        sent[base + spill : base + 2 * spill],
                    )
                )
                pieces.append(sent[base + 2 * spill : base + wire])
            sent = jnp.concatenate(pieces, axis=0)
        heat_send[...] = sent

        @pl.loop(1, n)
        def _(d):
            heat_copy(d).start()

        mine = pl.ds(pl.multiple_of(me * wire, wire), wire)
        heat_recv[mine] = heat_send[mine]

    def place_heat():
        @pl.loop(1, n)
        def _(d):
            heat_copy(d).wait_recv()

        got = heat_recv[...]
        if spill:
            spots = lax.broadcasted_iota(jnp.int32, (spill, tile), 1)
            pieces = []
            for p in range(n):
                message = got[p * wire : (p + 1) * wire]
                extra = jnp.where(
                    spots < half,
                    pltpu.roll(message[:spill], tile - levels, 1),
                    pltpu.roll(message[spill : 2 * spill], tile - levels + half, 1),
                )
                pieces += [message, extra]
            got = jnp.concatenate(pieces, axis=0)
        table = jnp.concatenate(split3(got.T), axis=0)
        placed = dot(table, to_slots[...])
        total = placed[:tile] + placed[tile : 2 * tile] + placed[2 * tile :]
        block_out[0] = total[:levels]

    work = [make_batch(b) for b in range(len(batches))]
    loads[0].wait()
    for batch in work:
        batch.pack(0, state)
    pl.semaphore_wait(barrier, n - 1)
    for batch in work:
        batch.start_halos(0)
    for load in loads[1:]:
        load.wait()
    for batch in work:
        batch.prepare()
    sort_columns()
    for t in range(STEPS):
        source = state if t == 0 else current
        for batch in work:
            batch.wait_halos(t)
            batch.advance(t, source)
            batch.analyse(t)
        if t == 0:
            ratios_of_levels()
        if t == STEPS - 1:
            place_columns()
        for batch in work:
            batch.own(t)
        carried = zeros
        for batch in work:
            batch.synthesise(t)
            if t + 1 < STEPS:
                batch.pack(t + 1, current)
                batch.start_halos(t + 1)
            else:
                carried = mix_down(batch, carried)
    mix_up()
    send_heat()
    for batch in work:
        for t in range(STEPS):
            batch.wait_sends(t)
    place_heat()

    @pl.loop(1, n)
    def _(d):
        slot_copy(d).wait_send()
        heat_copy(d).wait_send()


def split_levels(share, capacity):
    large = share - share // 2
    if large * capacity % 8 and large + 1 < share and (large + 1) * capacity % 8 == 0:
        large += 1
    return large, share - large


def program(n_lat, n_lon, capacity, state, mixing, insolation, filter_rows, block_map):
    fields, levels, rows, tile = state.shape
    n = n_lat * n_lon
    columns = rows * tile
    per_peer = columns // n
    rank = tile // fields
    large, small = split_levels(levels // n_lon, capacity)
    batches = ((0, large), (large * n_lon, small))
    analysis, between, synthesis = filter_tables(fields, tile, n_lon, rank)
    total_rows = rows * n_lat
    latitude = (np.arange(total_rows) + 0.5) * (math.pi / total_rows) - 0.5 * math.pi
    by_row = np.stack([1.0 / np.maximum(np.cos(latitude), FLOOR), np.sin(latitude)])
    by_row = by_row.reshape(2, n_lat, rows, 1).transpose(1, 0, 2, 3)
    geometry = np.broadcast_to(by_row, (n_lat, 2, rows, tile)).astype(np.float32)
    spare = per_peer % 32 == 0 and levels % 2 == 0 and levels + levels // 2 <= tile
    wire = per_peer * 3 // 4 if spare else per_peer
    vmem = pl.BlockSpec(memory_space=pltpu.VMEM)
    anywhere = pl.BlockSpec(memory_space=pl.ANY)
    sems = pltpu.SemaphoreType.DMA
    operands = (
        state,
        mixing,
        insolation,
        filter_rows,
        block_map,
        analysis,
        between,
        synthesis,
        geometry,
    )
    places = [
        pltpu.SMEM(a.shape, a.dtype) if a is filter_rows else pltpu.VMEM(a.shape, a.dtype)
        for a in operands
    ]
    per_batch = []
    for _, part in batches:
        count = part * n_lon
        edge = (STEPS, 2, fields, count, tile)
        side = (STEPS, 2, -(-count * fields // tile), rows, tile)
        many = -(-part * capacity // 8) * 8
        block = (STEPS, n_lon, many, tile)
        for shape in (edge, edge, side, side, block, block, block, block):
            per_batch.append(pltpu.VMEM(shape, F32))
        per_batch += [sems((STEPS, 4))] * 2 + [sems((STEPS, n_lon))] * 4
        per_batch.append(pltpu.VMEM((n_lon * many, count * rows), BF16))
        per_batch.append(pltpu.VMEM((count * rows, n_lon * many), BF16))
    return pl.pallas_call(
        functools.partial(kernel, n_lat, n_lon, batches, capacity),
        out_shape=(
            jax.ShapeDtypeStruct(state.shape, F32),
            jax.ShapeDtypeStruct((1, levels, columns), F32),
        ),
        in_specs=[anywhere] * len(operands),
        out_specs=(vmem, vmem),
        scratch_shapes=places
        + [
            sems((len(operands),)),
            pltpu.VMEM(state.shape, F32),
            pltpu.VMEM(state.shape, F32),
            pltpu.VMEM((levels, rows, tile), F32),
            pltpu.VMEM((levels, rows, tile), F32),
            pltpu.VMEM((levels, rows, tile), F32),
            pltpu.VMEM((columns, columns), BF16),
            pltpu.VMEM((columns, columns), BF16),
            pltpu.VMEM((3, tile, columns), BF16),
            pltpu.VMEM((n * wire, tile), F32),
            pltpu.VMEM((n * wire, tile), F32),
            pltpu.VMEM((n, 8, tile), F32),
            pltpu.VMEM((n, 8, tile), F32),
            sems((n,)),
            sems((n,)),
            sems((n,)),
            sems((n,)),
        ]
        + per_batch,
        compiler_params=pltpu.CompilerParams(
            collective_id=capacity, has_side_effects=True, vmem_limit_bytes=56 * 1024 * 1024
        ),
        cost_estimate=pl.CostEstimate(flops=8 * 10**9, bytes_accessed=6 * 10**6, transcendentals=0),
    )(*operands)


def per_device(n_lat, n_lon, state, mixing, insolation, filter_rows, block_map):
    rows = state.shape[2]
    capacities = (rows // 2, rows * 3 // 4, rows)
    band = lax.broadcasted_iota(jnp.int32, (n_lat, n_lat * rows), 1) // rows
    own_band = band == lax.broadcasted_iota(jnp.int32, band.shape, 0)
    most = jnp.max(jnp.sum(jnp.where(own_band, filter_rows[None], 0), axis=1))
    index = sum((most > limit).astype(jnp.int32) for limit in capacities[:-1])
    return lax.switch(
        index,
        [functools.partial(program, n_lat, n_lon, limit) for limit in capacities],
        state,
        mixing,
        insolation,
        filter_rows,
        block_map,
    )


def solution(mesh):
    n_lat, n_lon = mesh.shape["lat"], mesh.shape["lon"]
    in_specs = (P(None, None, "lat", "lon"), P("lat", "lon"), P("lat", "lon"), P(), P("lat", "lon"))
    out_specs = (P(None, None, "lat", "lon"), P(("lat", "lon"), None, None))
    return jax.shard_map(
        functools.partial(per_device, n_lat, n_lon),
        mesh=mesh,
        in_specs=in_specs,
        out_specs=out_specs,
        check_vma=False,
    )
```

```python
import functools
import math

import jax
import jax.numpy as jnp
import ml_dtypes
import numpy as np
from jax import lax
from jax.experimental import pallas as pl
from jax.experimental.pallas import tpu as pltpu
from jax.sharding import PartitionSpec as P

STEPS = 2
KEEP = 64
ADVECT = 0.1
DIFFUSE = 0.1
ROTATE = 0.2
RADIATE = 0.5
FLOOR = 0.25
MESH = pl.DeviceIdType.MESH
F32 = jnp.float32
BF16 = jnp.bfloat16


def filter_tables(fields, tile, n_lon, rank):
    total = tile * n_lon
    ids, waves = np.arange(tile), np.arange(KEEP)
    phase = 2 * np.pi * np.outer(ids, waves) / total
    basis = np.concatenate([np.cos(phase), np.sin(phase[:, 1:])], axis=1)
    basis = basis * np.sqrt(2 / total)
    basis[:, 0] /= np.sqrt(2)
    left = np.linalg.svd(basis, full_matrices=False)[0][:, :rank]
    between = np.zeros((n_lon, rank, n_lon, rank))
    for apart in range(-n_lon + 1, n_lon):
        gap = apart * tile + ids[:, None] - ids[None, :]
        kernel = np.ones(gap.shape) / total
        for wave in range(1, KEEP):
            kernel += (2 / total) * np.cos(2 * np.pi * ((wave * gap) % total) / total)
        block = left.T @ kernel @ left
        for source in range(n_lon):
            if 0 <= source + apart < n_lon:
                between[source, :, source + apart, :] = block.T
    lanes = fields * rank
    analysis = np.zeros((fields, tile, lanes))
    synthesis = np.zeros((lanes, fields, tile))
    for f in range(fields):
        analysis[f, :, f * rank : (f + 1) * rank] = left
        synthesis[f * rank : (f + 1) * rank, f, :] = left.T
    analysis = parts_of(analysis.reshape(fields * tile, lanes))
    between = parts_of(between.reshape(n_lon * rank, n_lon * rank))
    high, low = parts_of(synthesis.reshape(lanes, fields * tile))
    return (
        np.concatenate(analysis, axis=1),
        np.concatenate(between, axis=1),
        np.concatenate([high, high, low], axis=0),
    )


def parts_of(table):
    high = table.astype(ml_dtypes.bfloat16)
    return high, (table - high.astype(np.float64)).astype(ml_dtypes.bfloat16)


def split2(x):
    high = x.astype(BF16)
    return high, (x - high.astype(F32)).astype(BF16)


def dot(a, b):
    return jnp.dot(a, b, preferred_element_type=F32)


def dot_parts(x, table):
    width = table.shape[1] // 2
    high, low = split2(x)
    both = dot(high, table[...])
    return both[:, :width] + both[:, width:] + dot(low, table[:, :width])


def dot_nt(a, b):
    return lax.dot_general(a, b, (((1,), (1,)), ((), ())), preferred_element_type=F32)


def kernel(
    n_lat,
    n_lon,
    batches,
    capacity,
    state_in,
    mixing_in,
    sun_in,
    rows_in,
    map_in,
    analysis_in,
    between_in,
    synthesis_in,
    geometry_in,
    out,
    block_out,
    state,
    mixing,
    sun,
    wanted_rows,
    block_map,
    analysis,
    between,
    synthesis,
    geometry,
    in_sem,
    stepped,
    current,
    ratios,
    inverses,
    heat,
    to_sorted,
    to_slots,
    heat_split,
    heat_send,
    heat_recv,
    slot_send,
    slot_recv,
    slot_ssem,
    slot_rsem,
    heat_ssem,
    heat_rsem,
    *batch_refs,
):
    fields, levels, rows, tile = state.shape
    n = n_lat * n_lon
    columns = rows * tile
    per_peer = columns // n
    rank = tile // fields
    group = tile // fields
    wire = heat_send.shape[0] // n
    lat = lax.axis_index("lat")
    lon = lax.axis_index("lon")
    me = lat * n_lon + lon
    east = lax.rem(lon + 1, n_lon)
    west = lax.rem(lon + n_lon - 1, n_lon)

    sources = (
        state_in,
        mixing_in,
        sun_in,
        rows_in,
        map_in,
        analysis_in,
        between_in,
        synthesis_in,
        geometry_in,
    )
    places = (state, mixing, sun, wanted_rows, block_map, analysis, between, synthesis, geometry)
    loads = [
        pltpu.make_async_copy(src, dst, in_sem.at[k])
        for k, (src, dst) in enumerate(zip(sources, places))
    ]
    for load in loads:
        load.start()

    barrier = pltpu.get_barrier_semaphore()

    @pl.loop(1, n)
    def _(d):
        peer = lax.rem(me + d, n)
        pl.semaphore_signal(
            barrier, inc=1, device_id=(peer // n_lon, lax.rem(peer, n_lon)), device_id_type=MESH
        )

    lane = lax.broadcasted_iota(jnp.int32, (rows, tile), 1)
    row = lax.broadcasted_iota(jnp.int32, (rows, tile), 0)

    def ratio_of_level(l, upper):
        mix = mixing[...]
        at_end = jnp.logical_or(l == 0, l == levels - 1)
        diagonal = 1.0 + jnp.where(at_end, 1.0, 2.0) * mix
        inverse = 1.0 / (diagonal + mix * upper)
        ratio = -mix * inverse
        inverses[l] = inverse
        ratios[l] = ratio
        return ratio

    class Batch:
        pass

    def make_batch(b):
        first, share = batches[b]
        count = share * n_lon
        (
            lat_send,
            lat_recv,
            lon_send,
            lon_recv,
            z_send,
            z_recv,
            y_send,
            y_recv,
            halo_ssem,
            halo_rsem,
            z_ssem,
            z_rsem,
            y_ssem,
            y_rsem,
            pick,
            spread,
        ) = batch_refs[b * 16 : (b + 1) * 16]
        groups = lon_send.shape[2]
        here = pl.ds(first, count)
        many = z_send.shape[2]
        gathers = capacity < rows

        def one_hot(shape, packed_axis):
            packed = lax.broadcasted_iota(jnp.int32, shape, packed_axis)
            full = lax.broadcasted_iota(jnp.int32, shape, 1 - packed_axis)
            owner = packed // many
            inside = packed - owner * many
            level_in = inside // capacity
            spot = inside - level_in * capacity
            level = full // rows
            row_at = full - level * rows
            place = jnp.full(shape, -1, jnp.int32)
            taken = jnp.int32(0)
            for r in range(rows):
                used = wanted_rows[lat * rows + r]
                place = jnp.where(row_at == r, jnp.where(used == 1, taken, -1), place)
                taken = taken + used
            match = (level == owner * share + level_in) & (place == spot) & (level_in < share)
            return jnp.where(match, 1.0, 0.0).astype(BF16)

        def prepare():
            if gathers:
                pick[...] = one_hot(pick.shape, 0)
                spread[...] = one_hot(spread.shape, 1)

        def halo(t, side):
            if side < 2:
                src, dst = lat_send.at[t, side], lat_recv.at[t, side]
                peer = (lat + (1 if side == 0 else -1), lon)
            else:
                src, dst = lon_send.at[t, side - 2], lon_recv.at[t, side - 2]
                peer = (lat, east if side == 2 else west)
            return pltpu.make_async_remote_copy(
                src_ref=src,
                dst_ref=dst,
                send_sem=halo_ssem.at[t, side],
                recv_sem=halo_rsem.at[t, side],
                device_id=peer,
                device_id_type=MESH,
            )

        def pack(t, src):
            for f in range(fields):
                lat_send[t, 0, f] = src[f, here, rows - 1, :]
                lat_send[t, 1, f] = src[f, here, 0, :]
            for g in range(groups):
                lon_send[t, 0, g] = jnp.zeros((rows, tile), F32)
                lon_send[t, 1, g] = jnp.zeros((rows, tile), F32)
            chunk = math.gcd(math.gcd(count, group), 8)

            @pl.loop(0, count // chunk)
            def _(c):
                g = c * chunk // group
                low = lon_send[t, 1, g]
                high = lon_send[t, 0, g]
                for k in range(chunk):
                    l = c * chunk + k
                    for f in range(fields):
                        x = src[f, first + l]
                        spot = lane == lax.rem(l, group) * fields + f
                        low = jnp.where(spot, jnp.broadcast_to(x[:, :1], x.shape), low)
                        high = jnp.where(spot, jnp.broadcast_to(x[:, tile - 1 :], x.shape), high)
                lon_send[t, 1, g] = low
                lon_send[t, 0, g] = high

        def start_halos(t):
            halo(t, 2).start()
            halo(t, 3).start()

            @pl.when(lat < n_lat - 1)
            def _():
                halo(t, 0).start()

            @pl.when(lat > 0)
            def _():
                halo(t, 1).start()

        def wait_halos(t):
            @pl.when(lat > 0)
            def _():
                halo(t, 0).wait_recv()

            @pl.when(lat == 0)
            def _():
                lat_recv[t, 0] = jnp.zeros(lat_recv.shape[2:], F32)

            @pl.when(lat < n_lat - 1)
            def _():
                halo(t, 1).wait_recv()

            @pl.when(lat == n_lat - 1)
            def _():
                lat_recv[t, 1] = jnp.zeros(lat_recv.shape[2:], F32)

            halo(t, 2).wait_recv()
            halo(t, 3).wait_recv()

        def wait_halo_sends(t):
            @pl.when(lat < n_lat - 1)
            def _():
                halo(t, 0).wait_send()

            @pl.when(lat > 0)
            def _():
                halo(t, 1).wait_send()

            halo(t, 2).wait_send()
            halo(t, 3).wait_send()

        def advance(t, src, upper):
            metric = geometry[lat, 0]
            coriolis = geometry[lat, 1]

            def one(l):
                g = l // group
                from_west = lon_recv[t, 0, g]
                from_east = lon_recv[t, 1, g]
                u = src[0, first + l]
                v = src[1, first + l]
                zonal = u * metric
                made = []
                for f in range(fields):
                    x = src[f, first + l]
                    spot = lax.rem(l, group) * fields + f
                    eastern = jnp.where(
                        lane == tile - 1,
                        pltpu.roll(from_east, tile - 1 - spot, 1),
                        pltpu.roll(x, tile - 1, 1),
                    )
                    western = jnp.where(
                        lane == 0,
                        pltpu.roll(from_west, lax.rem(tile - spot, tile), 1),
                        pltpu.roll(x, 1, 1),
                    )
                    northern = jnp.where(
                        row == rows - 1,
                        lat_recv[t, 1, f, pl.ds(l, 1), :],
                        pltpu.roll(x, rows - 1, 0),
                    )
                    southern = jnp.where(
                        row == 0, lat_recv[t, 0, f, pl.ds(l, 1), :], pltpu.roll(x, 1, 0)
                    )
                    new = x - ADVECT * (zonal * (eastern - western) + v * (northern - southern))
                    new = new + DIFFUSE * (eastern + western + northern + southern - 4.0 * x)
                    if f == 0:
                        new = new + ROTATE * coriolis * v
                    if f == 1:
                        new = new - ROTATE * coriolis * u
                    made.append(new)
                return made

            chunk = math.gcd(count, 8)

            def some(c, upper):
                made = [one(c * chunk + k) for k in range(chunk)]
                for k in range(chunk):
                    if t == 0:
                        upper = ratio_of_level(first + c * chunk + k, upper)
                    for f in range(fields):
                        stepped[f, first + c * chunk + k] = made[k][f]
                return upper

            return lax.fori_loop(0, count // chunk, some, upper)

        def z_copy(t, d):
            owner = lax.rem(lon + d, n_lon)
            return pltpu.make_async_remote_copy(
                src_ref=z_send.at[t, owner],
                dst_ref=z_recv.at[t, lon],
                send_sem=z_ssem.at[t, d],
                recv_sem=z_rsem.at[t, d],
                device_id=(lat, owner),
                device_id_type=MESH,
            )

        def y_copy(t, d):
            source = lax.rem(lon + d, n_lon)
            return pltpu.make_async_remote_copy(
                src_ref=y_send.at[t, source],
                dst_ref=y_recv.at[t, lon],
                send_sem=y_ssem.at[t, d],
                recv_sem=y_rsem.at[t, d],
                device_id=(lat, source),
                device_id_type=MESH,
            )

        def analyse(t):
            parts = [stepped[f, here].reshape(count * rows, tile) for f in range(fields)]
            z = dot_parts(jnp.concatenate(parts, axis=1), analysis)
            if gathers:
                high, low = split2(z)
                z = dot(pick[...], high) + dot(pick[...], low)
            z_send[t] = z.reshape(n_lon, many, tile)

            @pl.loop(1, n_lon)
            def _(d):
                z_copy(t, d).start()

            z_recv[t, lon] = z_send[t, lon]

        def own(t):
            @pl.loop(1, n_lon)
            def _(d):
                z_copy(t, d).wait_recv()

            wide = lax.broadcasted_iota(jnp.int32, (many, tile), 1) // rank
            halves = []
            for h in range(n_lon // fields):
                got = [z_recv[t, h * fields + k] for k in range(fields)]
                per_field = []
                for f in range(fields):
                    total = None
                    for k in range(fields):
                        shift = (rank * (k - f)) % tile
                        moved = pltpu.roll(got[k], shift, 1) if shift else got[k]
                        total = moved if k == 0 else jnp.where(wide == k, moved, total)
                    per_field.append(total)
                halves.append(jnp.concatenate(per_field, axis=0))
            y = dot_parts(jnp.concatenate(halves, axis=1), between)
            for p in range(n_lon):
                h, k = p // fields, p % fields
                total = None
                for f in range(fields):
                    piece = y[f * many : (f + 1) * many, h * tile : (h + 1) * tile]
                    shift = (rank * (f - k)) % tile
                    piece = pltpu.roll(piece, shift, 1) if shift else piece
                    total = piece if f == 0 else jnp.where(wide == f, piece, total)
                y_send[t, p] = total

            @pl.loop(1, n_lon)
            def _(d):
                y_copy(t, d).start()

            y_recv[t, lon] = y_send[t, lon]

        def synthesise(t):
            wanted = jnp.zeros((rows, tile), jnp.int32)
            for r in range(rows):
                wanted = jnp.where(row == r, wanted_rows[lat * rows + r], wanted)
            filtered = (wanted == 1)[None]

            @pl.loop(1, n_lon)
            def _(d):
                y_copy(t, d).wait_recv()

            high, low = split2(y_recv[t].reshape(n_lon * many, tile))
            if gathers:
                high = dot(spread[...], high).astype(BF16)
                low = dot(spread[...], low).astype(BF16)
            smooth = dot(jnp.concatenate([high, low, high], axis=1), synthesis[...])
            for f in range(fields):
                piece = smooth[:, f * tile : (f + 1) * tile].reshape(count, rows, tile)
                current[f, here] = jnp.where(filtered, piece, stepped[f, here])

        def wait_sends(t):
            wait_halo_sends(t)

            @pl.loop(1, n_lon)
            def _(d):
                z_copy(t, d).wait_send()
                y_copy(t, d).wait_send()

        batch = Batch()
        batch.first, batch.count = first, count
        batch.pack, batch.start_halos, batch.wait_halos = pack, start_halos, wait_halos
        batch.advance, batch.analyse, batch.own = advance, analyse, own
        batch.synthesise, batch.wait_sends = synthesise, wait_sends
        batch.prepare = prepare
        return batch

    def slot_copy(d):
        peer = lax.rem(me + d, n)
        return pltpu.make_async_remote_copy(
            src_ref=slot_send.at[peer],
            dst_ref=slot_recv.at[me],
            send_sem=slot_ssem.at[d],
            recv_sem=slot_rsem.at[d],
            device_id=(peer // n_lon, lax.rem(peer, n_lon)),
            device_id_type=MESH,
        )

    def heat_copy(d):
        peer = lax.rem(me + d, n)
        there = pl.ds(pl.multiple_of(peer * wire, wire), wire)
        here = pl.ds(pl.multiple_of(me * wire, wire), wire)
        return pltpu.make_async_remote_copy(
            src_ref=heat_send.at[there],
            dst_ref=heat_recv.at[here],
            send_sem=heat_ssem.at[d],
            recv_sem=heat_rsem.at[d],
            device_id=(peer // n_lon, lax.rem(peer, n_lon)),
            device_id_type=MESH,
        )

    def sort_columns():
        mapped = block_map[...].astype(F32)
        target = jnp.floor((mapped + 0.5) * (1.0 / columns))
        slot = mapped - target * columns
        slot_high = slot.astype(BF16)
        slot_low = (slot - slot_high.astype(F32)).astype(BF16)
        peers = lax.broadcasted_iota(jnp.int32, (n, tile), 0).astype(F32)
        before = lax.broadcasted_iota(jnp.int32, (tile, tile), 0)
        after = lax.broadcasted_iota(jnp.int32, (tile, tile), 1)
        earlier = (before < after).astype(F32).astype(BF16)
        positions = lax.broadcasted_iota(jnp.int32, (columns, tile), 0).astype(F32)
        places = lax.broadcasted_iota(jnp.int32, (tile, tile), 0).astype(F32)
        base = jnp.zeros((n, 1), F32)
        slots = jnp.zeros((n, tile), F32)
        for r in range(rows):
            hit = (peers == target[r : r + 1]).astype(F32)
            prefix = dot(hit.astype(BF16), earlier) + base
            base = base + jnp.sum(hit, axis=1, keepdims=True)
            order = jnp.sum(hit * prefix, axis=0, keepdims=True)
            spot = target[r : r + 1] * per_peer + order
            to_sorted[:, r * tile : (r + 1) * tile] = (positions == spot).astype(F32).astype(BF16)
            named = (places == order).astype(F32)
            for part in (slot_high, slot_low):
                weighted = (named * part[r : r + 1].astype(F32)).astype(BF16)
                slots = slots + dot_nt(hit.astype(BF16), weighted)
        slot_send[...] = jnp.broadcast_to(slots[:, None, :], slot_send.shape)
        slot_recv[me] = slot_send[me]

        @pl.loop(1, n)
        def _(d):
            slot_copy(d).start()

    def place_columns():
        @pl.loop(1, n)
        def _(d):
            slot_copy(d).wait_recv()

        names = slot_recv[:, 0, :].T[:per_peer]
        join = max(1, 16 // per_peer)
        size = join * per_peer
        ids = lax.broadcasted_iota(jnp.int32, (size, columns), 1).astype(F32)
        for k in range(n // join):
            picked = [names[:, s : s + 1] for s in range(k * join, (k + 1) * join)]
            column = picked[0] if join == 1 else jnp.concatenate(picked, axis=0)
            to_slots[k * size : (k + 1) * size, :] = (ids == column).astype(F32).astype(BF16)

    zeros = tuple(jnp.zeros((rows, tile), F32) for f in range(fields))

    def mix_down(batch, carried):
        mix = mixing[...]

        def forward(l, above):
            inverse = inverses[l]
            values = tuple((current[f, l] + mix * above[f]) * inverse for f in range(fields))
            for f in range(fields):
                out[f, l] = values[f]
            return values

        return lax.fori_loop(batch.first, batch.first + batch.count, forward, carried, unroll=8)

    def mix_up():
        warming = RADIATE * sun[...]

        def backward(step, below):
            l = levels - 1 - step
            ratio = ratios[l]
            solved = tuple(out[f, l] - ratio * below[f] for f in range(fields))
            for f in range(fields):
                if f == 2:
                    warmed = solved[2] + warming * solved[3]
                    out[2, l] = warmed
                    heat[l] = warmed - current[2, l]
                else:
                    out[f, l] = solved[f]
            return solved

        lax.fori_loop(0, levels, backward, zeros, unroll=8)

    spill = per_peer - wire
    half = levels // 2

    def send_heat():
        for r in range(rows):
            for k, part in enumerate(split2(heat[:, r, :])):
                heat_split[k, :levels, r * tile : (r + 1) * tile] = part
                if levels < tile:
                    heat_split[k, levels:, r * tile : (r + 1) * tile] = jnp.zeros(
                        (tile - levels, tile), BF16
                    )
        table = heat_split[...].reshape(2 * tile, columns)
        sorted2 = dot_nt(to_sorted[...], table)
        sent = sorted2[:, :tile] + sorted2[:, tile:]
        if spill:
            spots = lax.broadcasted_iota(jnp.int32, (spill, tile), 1)
            free = spots >= levels
            pieces = []
            for p in range(n):
                base = p * per_peer
                extra = sent[base + wire : base + per_peer]
                pieces.append(
                    jnp.where(free, pltpu.roll(extra, levels, 1), sent[base : base + spill])
                )
                pieces.append(
                    jnp.where(
                        free,
                        pltpu.roll(extra, levels - half, 1),
                        sent[base + spill : base + 2 * spill],
                    )
                )
                pieces.append(sent[base + 2 * spill : base + wire])
            sent = jnp.concatenate(pieces, axis=0)
        heat_send[...] = sent

        @pl.loop(1, n)
        def _(d):
            heat_copy(d).start()

        mine = pl.ds(pl.multiple_of(me * wire, wire), wire)
        heat_recv[mine] = heat_send[mine]

    def place_heat():
        @pl.loop(1, n)
        def _(d):
            heat_copy(d).wait_recv()

        got = heat_recv[...]
        if spill:
            spots = lax.broadcasted_iota(jnp.int32, (spill, tile), 1)
            pieces = []
            for p in range(n):
                message = got[p * wire : (p + 1) * wire]
                extra = jnp.where(
                    spots < half,
                    pltpu.roll(message[:spill], tile - levels, 1),
                    pltpu.roll(message[spill : 2 * spill], tile - levels + half, 1),
                )
                pieces += [message, extra]
            got = jnp.concatenate(pieces, axis=0)
        table = jnp.concatenate(split2(got.T), axis=0)
        placed = dot(table, to_slots[...])
        total = placed[:tile] + placed[tile:]
        block_out[0] = total[:levels]

    work = [make_batch(b) for b in range(len(batches))]
    loads[0].wait()
    for batch in work:
        batch.pack(0, state)
    pl.semaphore_wait(barrier, n - 1)
    for batch in work:
        batch.start_halos(0)
    for load in loads[1:]:
        load.wait()
    for batch in work:
        batch.prepare()
    sort_columns()
    upper = zeros[0]
    for t in range(STEPS):
        source = state if t == 0 else current
        for batch in work:
            batch.wait_halos(t)
            upper = batch.advance(t, source, upper)
            batch.analyse(t)
        if t == STEPS - 1:
            place_columns()
        for batch in work:
            batch.own(t)
        carried = zeros
        for batch in work:
            batch.synthesise(t)
            if t + 1 < STEPS:
                batch.pack(t + 1, current)
                batch.start_halos(t + 1)
            else:
                carried = mix_down(batch, carried)
    mix_up()
    send_heat()
    for batch in work:
        for t in range(STEPS):
            batch.wait_sends(t)
    place_heat()

    @pl.loop(1, n)
    def _(d):
        slot_copy(d).wait_send()
        heat_copy(d).wait_send()


def split_levels(share, capacity):
    large = share - share // 2
    if large * capacity % 8 and large + 1 < share and (large + 1) * capacity % 8 == 0:
        large += 1
    return large, share - large


def program(n_lat, n_lon, capacity, state, mixing, insolation, filter_rows, block_map):
    fields, levels, rows, tile = state.shape
    n = n_lat * n_lon
    columns = rows * tile
    per_peer = columns // n
    rank = tile // fields
    large, small = split_levels(levels // n_lon, capacity)
    batches = ((0, large), (large * n_lon, small))
    analysis, between, synthesis = filter_tables(fields, tile, n_lon, rank)
    total_rows = rows * n_lat
    latitude = (np.arange(total_rows) + 0.5) * (math.pi / total_rows) - 0.5 * math.pi
    by_row = np.stack([1.0 / np.maximum(np.cos(latitude), FLOOR), np.sin(latitude)])
    by_row = by_row.reshape(2, n_lat, rows, 1).transpose(1, 0, 2, 3)
    geometry = np.broadcast_to(by_row, (n_lat, 2, rows, tile)).astype(np.float32)
    spare = per_peer % 32 == 0 and levels % 2 == 0 and levels + levels // 2 <= tile
    wire = per_peer * 3 // 4 if spare else per_peer
    vmem = pl.BlockSpec(memory_space=pltpu.VMEM)
    anywhere = pl.BlockSpec(memory_space=pl.ANY)
    sems = pltpu.SemaphoreType.DMA
    operands = (
        state,
        mixing,
        insolation,
        filter_rows,
        block_map,
        analysis,
        between,
        synthesis,
        geometry,
    )
    places = [
        pltpu.SMEM(a.shape, a.dtype) if a is filter_rows else pltpu.VMEM(a.shape, a.dtype)
        for a in operands
    ]
    per_batch = []
    for _, part in batches:
        count = part * n_lon
        edge = (STEPS, 2, fields, count, tile)
        side = (STEPS, 2, -(-count * fields // tile), rows, tile)
        many = -(-part * capacity // 8) * 8
        block = (STEPS, n_lon, many, tile)
        for shape in (edge, edge, side, side, block, block, block, block):
            per_batch.append(pltpu.VMEM(shape, F32))
        per_batch += [sems((STEPS, 4))] * 2 + [sems((STEPS, n_lon))] * 4
        per_batch.append(pltpu.VMEM((n_lon * many, count * rows), BF16))
        per_batch.append(pltpu.VMEM((count * rows, n_lon * many), BF16))
    return pl.pallas_call(
        functools.partial(kernel, n_lat, n_lon, batches, capacity),
        out_shape=(
            jax.ShapeDtypeStruct(state.shape, F32),
            jax.ShapeDtypeStruct((1, levels, columns), F32),
        ),
        in_specs=[anywhere] * len(operands),
        out_specs=(vmem, vmem),
        scratch_shapes=places
        + [
            sems((len(operands),)),
            pltpu.VMEM(state.shape, F32),
            pltpu.VMEM(state.shape, F32),
            pltpu.VMEM((levels, rows, tile), F32),
            pltpu.VMEM((levels, rows, tile), F32),
            pltpu.VMEM((levels, rows, tile), F32),
            pltpu.VMEM((columns, columns), BF16),
            pltpu.VMEM((columns, columns), BF16),
            pltpu.VMEM((2, tile, columns), BF16),
            pltpu.VMEM((n * wire, tile), F32),
            pltpu.VMEM((n * wire, tile), F32),
            pltpu.VMEM((n, 8, tile), F32),
            pltpu.VMEM((n, 8, tile), F32),
            sems((n,)),
            sems((n,)),
            sems((n,)),
            sems((n,)),
        ]
        + per_batch,
        compiler_params=pltpu.CompilerParams(
            collective_id=capacity, has_side_effects=True, vmem_limit_bytes=56 * 1024 * 1024
        ),
        cost_estimate=pl.CostEstimate(flops=8 * 10**9, bytes_accessed=6 * 10**6, transcendentals=0),
    )(*operands)


def per_device(n_lat, n_lon, state, mixing, insolation, filter_rows, block_map):
    rows = state.shape[2]
    capacities = (rows // 2, rows * 3 // 4, rows)
    band = lax.broadcasted_iota(jnp.int32, (n_lat, n_lat * rows), 1) // rows
    own_band = band == lax.broadcasted_iota(jnp.int32, band.shape, 0)
    most = jnp.max(jnp.sum(jnp.where(own_band, filter_rows[None], 0), axis=1))
    index = sum((most > limit).astype(jnp.int32) for limit in capacities[:-1])
    return lax.switch(
        index,
        [functools.partial(program, n_lat, n_lon, limit) for limit in capacities],
        state,
        mixing,
        insolation,
        filter_rows,
        block_map,
    )


def solution(mesh):
    n_lat, n_lon = mesh.shape["lat"], mesh.shape["lon"]
    in_specs = (P(None, None, "lat", "lon"), P("lat", "lon"), P("lat", "lon"), P(), P("lat", "lon"))
    out_specs = (P(None, None, "lat", "lon"), P(("lat", "lon"), None, None))
    return jax.shard_map(
        functools.partial(per_device, n_lat, n_lon),
        mesh=mesh,
        in_specs=in_specs,
        out_specs=out_specs,
        check_vma=False,
    )
```
